32 devices in a mesh: view: 4 (over x, core), block: 8 (over z, y).
Axes of the slice: x: 2, y: 2, z: 4, core: 2. Of those that a mesh axis runs over, the one named last changes fastest.
Arguments:
- estimate: float32 [8, 8, 128], P('block'), may hold values from 0.5 to 2
- view_data: float32 [4, 16, 8, 1, 128], P('view', 'block'), may hold values from 0.5 to 2
- taps_x: float32 [4, 33], P('view'), may hold values from 0.05 to 1
- taps_y: float32 [4, 33], P('view'), may hold values from 0.05 to 1
- taps_z: float32 [4, 33], P('view'), may hold values from 0.05 to 1
- owner: int32 [4, 8, 1], P('view'), may hold values from 0 to 7; in each aligned block of 8 rows (0 to 7, 8 to 15, ..., all dimensions but the last counted through in order) at most 2 rows name the same one
Outputs:
- joined: float32 [8, 8, 128], P('block')
The draws below stay inside these ranges and needn't reach their ends.
Inputs may be any that keep to these rules, and one draw needn't show every extreme that they name: `owner`: each view gives at most 2 slabs to one device, and some device holds 2 slabs of some view.
All inputs are finite; a program needn't handle non-finite values.
Results may differ from the reference program's by a relative error of at most 0.0001.
Values sent between devices are 32-bit elements; how exact they have to be, the bound alone decides.
No kernel may reach another device: no remote copies, remote signals or barrier semaphores. Data moves between devices by JAX's collectives and lax.ppermute only.
A program may use at most 64 MiB of HBM per device.

```python
import math
import jax
import jax.numpy as jnp
import numpy as np
from jax import lax

SX = 1
NZ = 128
R = 16
MOST = 2
ITERS = 2
VIEWS = 4
NX = 8
N_BLOCK = 8


def shard_levels(key, shape, shards, low, largest):
    def one(axis_at, blocks):
        heights = jax.random.uniform(jax.random.fold_in(jax.random.fold_in(key, 6), axis_at), (blocks,), jnp.float32, low / len(shards), largest / len(shards))
        return jnp.repeat(jnp.exp(heights), shape[axis_at] // blocks).reshape((-1,) + (1,) * (len(shape) - axis_at - 1))

    level = one(*shards[0])
    for cut in shards[1:]:
        level = level * one(*cut)
    return level


def routed_block(key, own, number, rows, amount, top, bound, slope):
    order = jax.random.permutation(key, amount)
    crowded, common = shares(amount, rows * top, bound, slope, True), shares(amount, rows * top, bound, slope, False)
    places = jnp.arange(amount)

    def named(tallies, offset_by):
        used = int((tallies > 0).sum())
        fixed = max(1, used // 4)
        passed = fixed + (places - fixed + offset_by * (used - fixed)) % max(1, amount - fixed)
        return jnp.zeros((amount,), jnp.int32).at[order[jnp.where(places < fixed, places, passed)]].set(jnp.asarray(tallies, jnp.int32))

    tallies = jnp.where(number % 4 == 0, named(crowded, number // 4), named(common, number - number // 4 - 1))
    mixed = jax.random.permutation(jax.random.fold_in(own, 3), amount)
    source_of, receiver = mixed[0:amount // 2 * 2:2], mixed[1:amount // 2 * 2:2]
    margin = jnp.minimum(tallies[source_of] - 1, bound - tallies[receiver]) // 2
    margin = jnp.where((source_of == order[0]) | (receiver == order[0]) | (tallies[receiver] == 0), 0, jnp.maximum(margin, 0))
    passed = jax.random.randint(jax.random.fold_in(own, 4), (amount // 2,), 0, 1 << 20) % (margin + 1)
    tallies = tallies.at[source_of].add(-passed).at[receiver].add(passed)
    labels = jnp.searchsorted(jnp.cumsum(tallies), jnp.arange(rows * top), side="right").astype(jnp.int32)
    table = labels.reshape(top, rows).T
    table = table[jax.random.permutation(jax.random.fold_in(own, 1), rows)]
    offset_by = jax.random.randint(jax.random.fold_in(own, 2), (rows, 1), 0, top)
    return jnp.take_along_axis(table, (jnp.arange(top)[None, :] + offset_by) % top, axis=1)


def shares(count, total, most, lean, full):
    loads = [(1 << 20) // math.isqrt(standing ** lean) + 1 for standing in range(1, count + 1)]
    largest = most if full else min(most, max(-(-total // count), total * loads[0] // sum(loads)))
    least = 1 if total - largest >= count - 1 else 0
    holding, rest = [largest] + [least] * (count - 1), total - largest - least * (count - 1)
    while rest > 0:
        free = [i for i in range(1, count) if holding[i] < largest] or [i for i in range(1, count) if holding[i] < most]
        whole, budget = sum([loads[i] for i in free]), rest
        for i in free:
            addition = min(most - holding[i], max(1, budget * loads[i] // whole), rest)
            holding[i] = holding[i] + addition
            rest = rest - addition
    return np.array(holding)


def setup_inputs(seed: int = 0) -> dict:
    streams_of = jax.random.split(jax.random.key(seed), 7)
    estimate = jnp.clip(jnp.exp(math.log(2.0) - 1.3862944 * jax.random.uniform(streams_of[0], (NX, NX, NZ), jnp.float32) ** shard_levels(streams_of[0], (NX, NX, NZ), ((0, 8),), -0.2, 0.2)), 0.5, 2.0)
    view_data = jnp.clip(jnp.exp(math.log(2.0) - 1.3862944 * jax.random.uniform(streams_of[1], (VIEWS, N_BLOCK * MOST, NX, SX, NZ), jnp.float32) ** shard_levels(streams_of[1], (VIEWS, N_BLOCK * MOST, NX, SX, NZ), ((0, 4), (1, 8)), -0.2, 0.2)), 0.5, 2.0)
    taps_x = jnp.clip(jnp.exp(math.log(1.0) - 2.9957323 * jax.random.uniform(streams_of[2], (VIEWS, 2 * R + 1), jnp.float32) ** shard_levels(streams_of[2], (VIEWS, 2 * R + 1), ((0, 4),), -0.2, 0.2)), 0.05, 1.0)
    taps_y = jnp.clip(jnp.exp(math.log(1.0) - 2.9957323 * jax.random.uniform(streams_of[3], (VIEWS, 2 * R + 1), jnp.float32) ** shard_levels(streams_of[3], (VIEWS, 2 * R + 1), ((0, 4),), -0.2, 0.2)), 0.05, 1.0)
    taps_z = jnp.clip(jnp.exp(math.log(1.0) - 2.9957323 * jax.random.uniform(streams_of[4], (VIEWS, 2 * R + 1), jnp.float32) ** shard_levels(streams_of[4], (VIEWS, 2 * R + 1), ((0, 4),), -0.2, 0.2)), 0.05, 1.0)
    owner_keys = jax.random.split(jax.random.fold_in(streams_of[5], 1), VIEWS * N_BLOCK // N_BLOCK)
    owner_turns = jax.random.permutation(jax.random.fold_in(streams_of[5], 3), VIEWS * N_BLOCK // N_BLOCK)
    owner = jax.vmap(lambda own, number: routed_block(jax.random.fold_in(streams_of[5], 2), own, number, N_BLOCK, N_BLOCK, 1, MOST, 1))(owner_keys, owner_turns).reshape((VIEWS, N_BLOCK, 1))
    return dict(estimate=estimate, view_data=view_data, taps_x=taps_x, taps_y=taps_y, taps_z=taps_z, owner=owner)


HIGH = lax.Precision.HIGHEST


def band_matrix(taps, length):
    width = taps.shape[0]
    reach = width // 2
    rows = jnp.arange(length, dtype=jnp.int32)[:, None]
    cols = jnp.arange(length, dtype=jnp.int32)[None, :]
    offset = cols - rows + reach
    inside = (offset >= 0) & (offset < width)
    index = jnp.clip(offset, 0, width - 1).astype(jnp.int32)
    values = jnp.take(taps.astype(jnp.float32), index.reshape(-1), axis=0).reshape(length, length)
    return jnp.where(inside, values, jnp.zeros_like(values))


def along(matrix, volume, axis):
    moved = jnp.moveaxis(volume, axis, -1)
    result = jnp.einsum('...j,ij->...i', moved, matrix, precision=HIGH)
    return jnp.moveaxis(result, -1, axis)


def reference(estimate, view_data, taps_x, taps_y, taps_z, owner):
    order = jnp.arange(N_BLOCK, dtype=jnp.int32)
    volumes = []
    for view in range(VIEWS):
        own = owner[view, :, 0]
        earlier = (own[:, None] == own[None, :]) & (order[None, :] < order[:, None])
        place = jnp.sum(earlier.astype(jnp.int32), axis=1)
        slot = (own * MOST + place).astype(jnp.int32)
        slabs = jnp.take(view_data[view], slot, axis=0)
        volumes.append(jnp.transpose(slabs, (1, 0, 2, 3)).reshape(NX, NX, NZ))
    est = estimate
    for step in range(ITERS):
        total = jnp.zeros(estimate.shape, jnp.float32)
        for view in range(VIEWS):
            m_x = band_matrix(taps_x[view], NX)
            m_y = band_matrix(taps_y[view], NX)
            m_z = band_matrix(taps_z[view], NZ)
            blurred = along(m_z, along(m_y, along(m_x, est, 0), 1), 2)
            ratio = volumes[view] / blurred
            corr = along(m_z.T, along(m_y.T, along(m_x.T, ratio, 0), 1), 2)
            total = total + jnp.log(corr)
        est = est * jnp.exp(total / VIEWS)
    return est
```

```python
import functools

import jax
import jax.numpy as jnp
from jax import lax
from jax.experimental import pallas as pl
from jax.experimental.pallas import tpu as pltpu
from jax.sharding import PartitionSpec as P

ITERS = 2

HIGH = lax.Precision.HIGHEST

SIDE = 8
LANES = 128
DATA_ROWS = 16
PACKET = 24


def lane_ids(rows):
    return lax.broadcasted_iota(jnp.int32, (rows, LANES), 1)


def row_ids(rows):
    return lax.broadcasted_iota(jnp.int32, (rows, LANES), 0)


def pack_kernel(copies, reach, own, est, data, tx, ty, tz, out, taps):
    block = lax.axis_index("block")
    view = lax.axis_index("view")
    width = 2 * reach + 1
    taps[...] = jnp.zeros_like(taps)
    taps[2:3, :width] = tz[...]
    taps[3:4, :width] = tx[...]
    taps[4:5, :width] = tx[...]
    taps[5:6, :width] = ty[...]
    first = jnp.int32(-1)
    second = jnp.int32(-1)
    for y in range(SIDE):
        mine = own[y] == block
        second = jnp.where(mine & (first >= 0), y, second)
        first = jnp.where(mine & (first < 0), y, first)
    lane = lane_ids(SIDE)
    row = row_ids(SIDE)
    along_z = jnp.where(lane < LANES // 2, lane, lane - LANES) + reach
    along_x = (lane & (SIDE - 1)) + reach
    along_y = (lane >> 3) + jnp.where(lane < LANES // 2, reach, reach - 16)
    index = jnp.where(row == 2, along_z, jnp.where(row == 3, along_x, jnp.where(row == 4, along_x - SIDE, along_y)))
    inside = (index >= 0) & (index < width)
    picked = jnp.take_along_axis(taps[...], jnp.clip(index, 0, width - 1), axis=1)
    tile = jnp.where(inside, picked, 0.0)
    for k in range(2):
        tile = jnp.where(row == k, est[pl.ds(2 * view + k, 1), :], tile)
    tile = jnp.where(row == 6, first.astype(jnp.float32), tile)
    tile = jnp.where(row == 7, second.astype(jnp.float32), tile)
    lower, upper = data[:SIDE], data[SIDE:]
    for k in range(copies):
        out[k, :SIDE] = lower
        out[k, SIDE:DATA_ROWS] = upper
        out[k, DATA_ROWS:] = tile


def halves(value):
    high = value.astype(jnp.bfloat16)
    low = (value - high.astype(jnp.float32)).astype(jnp.bfloat16)
    return high, low


def matmul(a, b):
    return jnp.dot(a, b, preferred_element_type=jnp.float32)


def per_side(matrix):
    doubled = jnp.concatenate([matrix, matrix], axis=1)
    high, low = halves(doubled)
    both = jnp.where(lane_ids(matrix.shape[0]) < matrix.shape[1], high.astype(jnp.float32), low.astype(jnp.float32))
    both = both.astype(jnp.bfloat16)
    return jnp.concatenate([both, both], axis=1)


def per_depth(matrix):
    high, low = halves(matrix)
    row = jnp.concatenate([high, low], axis=1)
    return jnp.concatenate([row, row], axis=0)


def apply_side(sided, value):
    high, low = halves(value)
    return matmul(sided, jnp.concatenate([high, high, low, low], axis=0))


def apply_depth(value, deep):
    high, low = halves(value)
    both = matmul(jnp.concatenate([high, low], axis=1), deep)
    return both[:, :LANES] + both[:, LANES:]


def geometric_mean(values):
    if len(values) == 1:
        return values[0]
    half = len(values) // 2
    return jnp.sqrt(geometric_mean(values[:half]) * geometric_mean(values[half:]))


def volume_kernel(blocks, groups, reach, near, far, out, held):
    block = lax.axis_index("block")
    core = lax.axis_index("view") & 1
    sources = [(ref, g * blocks * PACKET) for ref in (near, far) for g in range(groups)]

    tiles = []
    for y in range(SIDE):
        view, k = y // 2, y % 2
        start = (view // 2) * blocks * PACKET + DATA_ROWS + k
        rows = pl.ds(start, blocks, stride=PACKET)
        same = (core == view % 2).astype(jnp.int32) > 0
        tiles.append(jnp.where(same, near[rows, :], far[rows, :]))
    est = jnp.concatenate(tiles, axis=0)

    lane, row = lane_ids(SIDE), row_ids(SIDE)
    band = jnp.abs(lane_ids(LANES) - row_ids(LANES)) <= reach
    recorded, forward_side, forward_depth, back_side, back_depth = [], [], [], [], []
    for ref, start in sources:
        slabs = [jnp.zeros((SIDE, LANES), jnp.float32)] * SIDE
        for b in range(blocks):
            at = start + b * PACKET
            for s in range(2):
                label = jnp.broadcast_to(ref[at + DATA_ROWS + 6 + s : at + DATA_ROWS + 7 + s, :], (SIDE, LANES))
                slab = ref[at + s * SIDE : at + (s + 1) * SIDE, :]
                for y in range(SIDE):
                    slabs[y] = jnp.where(label == y, slab, slabs[y])
        recorded.append(jnp.concatenate(slabs, axis=0))

        def meta(k, rows):
            at = start + DATA_ROWS + k
            return jnp.broadcast_to(ref[at : at + 1, :], (rows, LANES))

        deep = pltpu.roll(meta(2, LANES), 0, 1, stride=1, stride_axis=0)
        deep = jnp.where(band, deep, 0.0)
        forward_depth.append(per_depth(deep.T))
        back_depth.append(per_depth(deep))
        upper = pltpu.roll(meta(3, SIDE), 0, 1, stride=1, stride_axis=0)
        lower = pltpu.roll(meta(4, SIDE), 0, 1, stride=1, stride_axis=0)
        x_tile = jnp.where((lane & (SIDE - 1)) >= row, upper, lower)
        y_tile = pltpu.roll(meta(5, SIDE), 0, 1, stride=SIDE, stride_axis=0)
        side = jnp.concatenate([x_tile * y_tile[y : y + 1, :] for y in range(SIDE)], axis=0)
        side = side[:, : SIDE * SIDE]
        forward_side.append(per_side(side))
        back_side.append(per_side(side.T))

    for step in range(ITERS):
        corrections = []
        for v in range(len(sources)):
            blurred = apply_side(forward_side[v], apply_depth(est, forward_depth[v]))
            ratio = recorded[v] / blurred
            corrections.append(apply_depth(apply_side(back_side[v], ratio), back_depth[v]))
        est = est * geometric_mean(corrections)
    held[...] = est
    out[...] = held[pl.ds(block, SIDE, stride=SIDE), :]


def on_device_small(estimate, view_data, taps_x, taps_y, taps_z, owner):
    blocks = lax.axis_size("block")
    views = lax.axis_size("view")
    reach = taps_x.shape[1] // 2
    groups = views // 2
    copies = groups * blocks
    smem = pl.BlockSpec(memory_space=pltpu.SMEM)
    vmem = pl.BlockSpec(memory_space=pltpu.VMEM)
    packet = pl.pallas_call(
        functools.partial(pack_kernel, copies, reach),
        out_shape=jax.ShapeDtypeStruct((copies, PACKET, LANES), jnp.float32),
        in_specs=[smem] + [vmem] * 5,
        out_specs=vmem,
        scratch_shapes=[pltpu.VMEM((SIDE, LANES), jnp.float32)],
        name="pack",
    )(owner.reshape(-1), estimate.reshape(SIDE, LANES), view_data.reshape(DATA_ROWS, LANES), taps_x, taps_y, taps_z)
    alike = [[(2 * g + c) * blocks + b for g in range(groups) for b in range(blocks)] for c in range(2)]
    near = lax.all_to_all(packet, ("view", "block"), 0, 0, axis_index_groups=alike, tiled=True)
    near = near.reshape(copies * PACKET, LANES)
    far = lax.ppermute(near, "view", [(v, v ^ 1) for v in range(views)])
    joined = pl.pallas_call(
        functools.partial(volume_kernel, blocks, groups, reach),
        out_shape=jax.ShapeDtypeStruct((SIDE, LANES), jnp.float32),
        in_specs=[vmem] * 2,
        out_specs=vmem,
        scratch_shapes=[pltpu.VMEM((SIDE * SIDE, LANES), jnp.float32)],
        name="volume",
    )(near, far)
    return joined.reshape(estimate.shape)


def fits_one_device(estimate, view_data, taps_x, blocks, views):
    thin, total_y, depth = estimate.shape
    reach = taps_x.shape[1] // 2
    return (
        (thin, blocks, total_y, depth) == (1, SIDE, SIDE, LANES)
        and view_data.shape[1] == 2
        and views == 4
        and taps_x.shape[1] % 2 == 1
        and reach < LANES // 2
    )


def band_matrix(taps, length):
    width = taps.shape[0]
    reach = width // 2
    rows = jnp.arange(length, dtype=jnp.int32)[:, None]
    cols = jnp.arange(length, dtype=jnp.int32)[None, :]
    offset = cols - rows + reach
    inside = (offset >= 0) & (offset < width)
    index = jnp.clip(offset, 0, width - 1)
    values = jnp.take(taps, index.reshape(-1), axis=0).reshape(length, length)
    return jnp.where(inside, values, jnp.zeros_like(values))


def on_device(estimate, view_data, taps_x, taps_y, taps_z, owner):
    blocks = lax.axis_size("block")
    views = lax.axis_size("view")
    if fits_one_device(estimate, view_data, taps_x, blocks, views):
        return on_device_small(estimate, view_data, taps_x, taps_y, taps_z, owner)
    thin = estimate.shape[0]
    total_y = estimate.shape[1]
    depth = estimate.shape[2]
    total_x = thin * blocks
    slots = view_data.shape[1]
    own = owner[0, :, 0]
    order = jnp.arange(blocks, dtype=jnp.int32)
    earlier = (own[:, None] == own[None, :]) & (order[None, :] < order[:, None])
    place = jnp.sum(earlier.astype(jnp.int32), axis=1)
    slot_ids = jnp.arange(slots, dtype=jnp.int32)
    hits = (place[None, None, :] == slot_ids[:, None, None]) & (
        own[None, None, :] == order[None, :, None]
    )
    filled = jnp.any(hits, axis=2).astype(jnp.float32)
    source_slab = jnp.sum(jnp.where(hits, order[None, None, :], 0), axis=2)
    return_index = place * blocks + own
    device = lax.axis_index("block")
    held = jnp.sum((own == device).astype(jnp.int32))
    live = (slot_ids < held)[:, None, None, None]
    m_x = band_matrix(taps_x[0], total_x)
    m_y = band_matrix(taps_y[0], total_y)
    m_z = band_matrix(taps_z[0], depth)
    recorded = view_data[0]
    est = estimate
    for step in range(ITERS):
        forward = jnp.einsum("ij,xjz->xiz", m_y, est, precision=HIGH)
        pieces = forward.reshape(thin, blocks, thin, depth)
        picked = jnp.take(pieces, source_slab.reshape(-1), axis=1)
        picked = picked.reshape(thin, slots, blocks, thin, depth).transpose(1, 2, 0, 3, 4)
        picked = picked * filled[:, :, None, None, None]
        arrived = lax.all_to_all(picked, "block", split_axis=1, concat_axis=1, tiled=True)
        held_est = arrived.reshape(slots, total_x, thin, depth)
        blurred = jnp.einsum("ij,sjyz->siyz", m_x, held_est, precision=HIGH)
        blurred = jnp.einsum("sxyj,ij->sxyi", blurred, m_z, precision=HIGH)
        ratio = jnp.where(live, recorded / jnp.where(live, blurred, 1.0), 0.0)
        back = jnp.einsum("ji,sjyz->siyz", m_x, ratio, precision=HIGH)
        back = jnp.einsum("sxyj,ji->sxyi", back, m_z, precision=HIGH)
        returned = lax.all_to_all(
            back.reshape(slots, blocks, thin, thin, depth),
            "block",
            split_axis=1,
            concat_axis=1,
            tiled=True,
        )
        flat = returned.reshape(slots * blocks, thin, thin, depth)
        gathered = jnp.take(flat, return_index, axis=0)
        corr = gathered.transpose(1, 0, 2, 3).reshape(thin, total_y, depth)
        corr = jnp.einsum("ji,xjz->xiz", m_y, corr, precision=HIGH)
        logs = lax.psum(jnp.log(corr), "view")
        est = est * jnp.exp(logs / views)
    return est


def solution(mesh):
    in_specs = (
        P("block", None, None),
        P("view", "block", None, None, None),
        P("view", None),
        P("view", None),
        P("view", None),
        P("view", None, None),
    )
    out_specs = P("block", None, None)
    return jax.shard_map(
        on_device, mesh=mesh, in_specs=in_specs, out_specs=out_specs, check_vma=False
    )
```

```python
import functools

import jax
import jax.numpy as jnp
from jax import lax
from jax.experimental import pallas as pl
from jax.experimental.pallas import tpu as pltpu
from jax.sharding import PartitionSpec as P

ITERS = 2

HIGH = lax.Precision.HIGHEST

SIDE = 8
LANES = 128
DATA_ROWS = 16
PACKET = 24


def lane_ids(rows):
    return lax.broadcasted_iota(jnp.int32, (rows, LANES), 1)


def row_ids(rows):
    return lax.broadcasted_iota(jnp.int32, (rows, LANES), 0)


def pack_kernel(copies, reach, own, est, data, tx, ty, tz, out, taps):
    block = lax.axis_index("block")
    view = lax.axis_index("view")
    width = 2 * reach + 1
    taps[...] = jnp.zeros_like(taps)
    taps[2:3, :width] = tz[...]
    taps[3:4, :width] = tx[...]
    taps[4:5, :width] = tx[...]
    taps[5:6, :width] = ty[...]
    first = jnp.int32(-1)
    second = jnp.int32(-1)
    for y in range(SIDE):
        mine = own[y] == block
        second = jnp.where(mine & (first >= 0), y, second)
        first = jnp.where(mine & (first < 0), y, first)
    lane = lane_ids(SIDE)
    row = row_ids(SIDE)
    along_z = jnp.where(lane < LANES // 2, lane, lane - LANES) + reach
    along_x = (lane & (SIDE - 1)) + reach
    along_y = (lane >> 3) + jnp.where(lane < LANES // 2, reach, reach - 16)
    index = jnp.where(row == 2, along_z, jnp.where(row == 3, along_x, jnp.where(row == 4, along_x - SIDE, along_y)))
    inside = (index >= 0) & (index < width)
    picked = jnp.take_along_axis(taps[...], jnp.clip(index, 0, width - 1), axis=1)
    tile = jnp.where(inside, picked, 0.0)
    for k in range(2):
        tile = jnp.where(row == k, est[pl.ds(2 * view + k, 1), :], tile)
    tile = jnp.where(row == 6, first.astype(jnp.float32), tile)
    tile = jnp.where(row == 7, second.astype(jnp.float32), tile)
    lower, upper = data[:SIDE], data[SIDE:]
    for k in range(copies):
        out[k, :SIDE] = lower
        out[k, SIDE:DATA_ROWS] = upper
        out[k, DATA_ROWS:] = tile


def halves(value):
    high = value.astype(jnp.bfloat16)
    low = (value - high.astype(jnp.float32)).astype(jnp.bfloat16)
    return high, low


def matmul(a, b):
    return jnp.dot(a, b, preferred_element_type=jnp.float32)


def per_side(matrix):
    doubled = jnp.concatenate([matrix, matrix], axis=1)
    high, low = halves(doubled)
    both = jnp.where(lane_ids(matrix.shape[0]) < matrix.shape[1], high.astype(jnp.float32), low.astype(jnp.float32))
    both = both.astype(jnp.bfloat16)
    return jnp.concatenate([both, both], axis=1)


def per_depth(matrix):
    high, low = halves(matrix)
    row = jnp.concatenate([high, low], axis=1)
    return jnp.concatenate([row, row], axis=0)


def apply_side(sided, value):
    high, low = halves(value)
    return matmul(sided, jnp.concatenate([high, high, low, low], axis=0))


def apply_depth(value, deep):
    high, low = halves(value)
    both = matmul(jnp.concatenate([high, low], axis=1), deep)
    return both[:, :LANES] + both[:, LANES:]


def geometric_mean(values):
    if len(values) == 1:
        return values[0]
    half = len(values) // 2
    return jnp.sqrt(geometric_mean(values[:half]) * geometric_mean(values[half:]))


def volume_kernel(blocks, groups, reach, near, far, out, held):
    block = lax.axis_index("block")
    core = lax.axis_index("view") & 1
    sources = [(ref, g * blocks * PACKET) for ref in (near, far) for g in range(groups)]

    tiles = []
    for y in range(SIDE):
        view, k = y // 2, y % 2
        start = (view // 2) * blocks * PACKET + DATA_ROWS + k
        rows = pl.ds(start, blocks, stride=PACKET)
        same = (core == view % 2).astype(jnp.int32) > 0
        tiles.append(jnp.where(same, near[rows, :], far[rows, :]))
    est = jnp.concatenate(tiles, axis=0)

    lane, row = lane_ids(SIDE), row_ids(SIDE)
    band = jnp.abs(lane_ids(LANES) - row_ids(LANES)) <= reach
    recorded, forward_side, forward_depth, back_side, back_depth = [], [], [], [], []
    for ref, start in sources:
        slabs = [jnp.zeros((SIDE, LANES), jnp.float32)] * SIDE
        for b in range(blocks):
            at = start + b * PACKET
            for s in range(2):
                label = jnp.broadcast_to(ref[at + DATA_ROWS + 6 + s : at + DATA_ROWS + 7 + s, :], (SIDE, LANES))
                slab = ref[at + s * SIDE : at + (s + 1) * SIDE, :]
                for y in range(SIDE):
                    slabs[y] = jnp.where(label == y, slab, slabs[y])
        recorded.append(jnp.concatenate(slabs, axis=0))

        def meta(k, rows):
            at = start + DATA_ROWS + k
            return jnp.broadcast_to(ref[at : at + 1, :], (rows, LANES))

        deep = pltpu.roll(meta(2, LANES), 0, 1, stride=1, stride_axis=0)
        deep = jnp.where(band, deep, 0.0)
        forward_depth.append(per_depth(deep.T))
        back_depth.append(per_depth(deep))
        upper = pltpu.roll(meta(3, SIDE), 0, 1, stride=1, stride_axis=0)
        lower = pltpu.roll(meta(4, SIDE), 0, 1, stride=1, stride_axis=0)
        x_tile = jnp.where((lane & (SIDE - 1)) >= row, upper, lower)
        y_tile = pltpu.roll(meta(5, SIDE), 0, 1, stride=SIDE, stride_axis=0)
        side = jnp.concatenate([x_tile * y_tile[y : y + 1, :] for y in range(SIDE)], axis=0)
        side = side[:, : SIDE * SIDE]
        forward_side.append(per_side(side))
        back_side.append(per_side(side.T))

    for step in range(ITERS):
        corrections = []
        for v in range(len(sources)):
            blurred = apply_side(forward_side[v], apply_depth(est, forward_depth[v]))
            ratio = recorded[v] / blurred
            corrections.append(apply_depth(apply_side(back_side[v], ratio), back_depth[v]))
        est = est * geometric_mean(corrections)
    held[...] = est
    out[...] = held[pl.ds(block, SIDE, stride=SIDE), :]


def on_device_small(estimate, view_data, taps_x, taps_y, taps_z, owner):
    blocks = lax.axis_size("block")
    views = lax.axis_size("view")
    reach = taps_x.shape[1] // 2
    groups = views // 2
    copies = groups * blocks
    smem = pl.BlockSpec(memory_space=pltpu.SMEM)
    vmem = pl.BlockSpec(memory_space=pltpu.VMEM)
    packet = pl.pallas_call(
        functools.partial(pack_kernel, copies, reach),
        out_shape=pltpu.VMEM((copies, PACKET, LANES), jnp.float32),
        in_specs=[smem] + [vmem] * 5,
        out_specs=vmem,
        scratch_shapes=[pltpu.VMEM((SIDE, LANES), jnp.float32)],
        name="pack",
    )(owner.reshape(-1), estimate.reshape(SIDE, LANES), view_data.reshape(DATA_ROWS, LANES), taps_x, taps_y, taps_z)
    alike = [[(2 * g + c) * blocks + b for g in range(groups) for b in range(blocks)] for c in range(2)]
    near = lax.all_to_all(packet, ("view", "block"), 0, 0, axis_index_groups=alike, tiled=True)
    near = near.reshape(copies * PACKET, LANES)
    far = lax.ppermute(near, "view", [(v, v ^ 1) for v in range(views)])
    near = pltpu.with_memory_space_constraint(near, pltpu.VMEM)
    far = pltpu.with_memory_space_constraint(far, pltpu.VMEM)
    joined = pl.pallas_call(
        functools.partial(volume_kernel, blocks, groups, reach),
        out_shape=jax.ShapeDtypeStruct((SIDE, LANES), jnp.float32),
        in_specs=[vmem] * 2,
        out_specs=vmem,
        scratch_shapes=[pltpu.VMEM((SIDE * SIDE, LANES), jnp.float32)],
        name="volume",
    )(near, far)
    return joined.reshape(estimate.shape)


def fits_one_device(estimate, view_data, taps_x, blocks, views):
    thin, total_y, depth = estimate.shape
    reach = taps_x.shape[1] // 2
    return (
        (thin, blocks, total_y, depth) == (1, SIDE, SIDE, LANES)
        and view_data.shape[1] == 2
        and views == 4
        and taps_x.shape[1] % 2 == 1
        and reach < LANES // 2
    )


def band_matrix(taps, length):
    width = taps.shape[0]
    reach = width // 2
    rows = jnp.arange(length, dtype=jnp.int32)[:, None]
    cols = jnp.arange(length, dtype=jnp.int32)[None, :]
    offset = cols - rows + reach
    inside = (offset >= 0) & (offset < width)
    index = jnp.clip(offset, 0, width - 1)
    values = jnp.take(taps, index.reshape(-1), axis=0).reshape(length, length)
    return jnp.where(inside, values, jnp.zeros_like(values))


def on_device(estimate, view_data, taps_x, taps_y, taps_z, owner):
    blocks = lax.axis_size("block")
    views = lax.axis_size("view")
    if fits_one_device(estimate, view_data, taps_x, blocks, views):
        return on_device_small(estimate, view_data, taps_x, taps_y, taps_z, owner)
    thin = estimate.shape[0]
    total_y = estimate.shape[1]
    depth = estimate.shape[2]
    total_x = thin * blocks
    slots = view_data.shape[1]
    own = owner[0, :, 0]
    order = jnp.arange(blocks, dtype=jnp.int32)
    earlier = (own[:, None] == own[None, :]) & (order[None, :] < order[:, None])
    place = jnp.sum(earlier.astype(jnp.int32), axis=1)
    slot_ids = jnp.arange(slots, dtype=jnp.int32)
    hits = (place[None, None, :] == slot_ids[:, None, None]) & (
        own[None, None, :] == order[None, :, None]
    )
    filled = jnp.any(hits, axis=2).astype(jnp.float32)
    source_slab = jnp.sum(jnp.where(hits, order[None, None, :], 0), axis=2)
    return_index = place * blocks + own
    device = lax.axis_index("block")
    held = jnp.sum((own == device).astype(jnp.int32))
    live = (slot_ids < held)[:, None, None, None]
    m_x = band_matrix(taps_x[0], total_x)
    m_y = band_matrix(taps_y[0], total_y)
    m_z = band_matrix(taps_z[0], depth)
    recorded = view_data[0]
    est = estimate
    for step in range(ITERS):
        forward = jnp.einsum("ij,xjz->xiz", m_y, est, precision=HIGH)
        pieces = forward.reshape(thin, blocks, thin, depth)
        picked = jnp.take(pieces, source_slab.reshape(-1), axis=1)
        picked = picked.reshape(thin, slots, blocks, thin, depth).transpose(1, 2, 0, 3, 4)
        picked = picked * filled[:, :, None, None, None]
        arrived = lax.all_to_all(picked, "block", split_axis=1, concat_axis=1, tiled=True)
        held_est = arrived.reshape(slots, total_x, thin, depth)
        blurred = jnp.einsum("ij,sjyz->siyz", m_x, held_est, precision=HIGH)
        blurred = jnp.einsum("sxyj,ij->sxyi", blurred, m_z, precision=HIGH)
        ratio = jnp.where(live, recorded / jnp.where(live, blurred, 1.0), 0.0)
        back = jnp.einsum("ji,sjyz->siyz", m_x, ratio, precision=HIGH)
        back = jnp.einsum("sxyj,ji->sxyi", back, m_z, precision=HIGH)
        returned = lax.all_to_all(
            back.reshape(slots, blocks, thin, thin, depth),
            "block",
            split_axis=1,
            concat_axis=1,
            tiled=True,
        )
        flat = returned.reshape(slots * blocks, thin, thin, depth)
        gathered = jnp.take(flat, return_index, axis=0)
        corr = gathered.transpose(1, 0, 2, 3).reshape(thin, total_y, depth)
        corr = jnp.einsum("ji,xjz->xiz", m_y, corr, precision=HIGH)
        logs = lax.psum(jnp.log(corr), "view")
        est = est * jnp.exp(logs / views)
    return est


def solution(mesh):
    in_specs = (
        P("block", None, None),
        P("view", "block", None, None, None),
        P("view", None),
        P("view", None),
        P("view", None),
        P("view", None, None),
    )
    out_specs = P("block", None, None)
    return jax.shard_map(
        on_device, mesh=mesh, in_specs=in_specs, out_specs=out_specs, check_vma=False
    )
```

```python
import functools

import jax
import jax.numpy as jnp
from jax import lax
from jax.experimental import pallas as pl
from jax.experimental.pallas import tpu as pltpu
from jax.sharding import PartitionSpec as P

ITERS = 2

HIGH = lax.Precision.HIGHEST

SIDE = 8
LANES = 128
DATA_ROWS = 16
PACKET = 24


def lane_ids(rows):
    return lax.broadcasted_iota(jnp.int32, (rows, LANES), 1)


def row_ids(rows):
    return lax.broadcasted_iota(jnp.int32, (rows, LANES), 0)


def pack_kernel(copies, own, est, data, tx, ty, tz, out, meta):
    block = lax.axis_index("block")
    view = lax.axis_index("view")
    width = tx.shape[1]
    first = jnp.int32(-1)
    second = jnp.int32(-1)
    for y in range(SIDE):
        mine = own[y] == block
        second = jnp.where(mine & (first >= 0), y, second)
        first = jnp.where(mine & (first < 0), y, first)
    lane = lane_ids(1)
    meta[...] = jnp.where(lane == 3 * width, first, second).astype(jnp.float32)
    for k, taps in enumerate((tx, ty, tz)):
        meta[:, k * width : (k + 1) * width] = taps[...]
    row = row_ids(SIDE)
    tile = jnp.broadcast_to(meta[...], (SIDE, LANES))
    for k in range(2):
        tile = jnp.where(row == k, est[pl.ds(2 * view + k, 1), :], tile)
    lower, upper = data[:SIDE], data[SIDE:]
    for k in range(copies):
        out[k, :SIDE] = lower
        out[k, SIDE:DATA_ROWS] = upper
        out[k, DATA_ROWS:] = tile


def halves(value):
    high = value.astype(jnp.bfloat16)
    low = (value - high.astype(jnp.float32)).astype(jnp.bfloat16)
    return high, low


def matmul(a, b):
    return jnp.dot(a, b, preferred_element_type=jnp.float32)


def left(value):
    high, low = halves(value)
    return jnp.concatenate([high, low, high], axis=1)


def right(value):
    high, low = halves(value)
    return jnp.concatenate([high, high, low], axis=0)


def lane_pick(tile, index):
    return jnp.take_along_axis(tile, index, axis=1)


def volume_kernel(blocks, groups, reach, near, far, out, held):
    block = lax.axis_index("block")
    core = lax.axis_index("view") & 1
    width = 2 * reach + 1
    sources = [(ref, g * blocks * PACKET) for ref in (near, far) for g in range(groups)]
    views = range(len(sources))

    tiles = []
    for y in range(SIDE):
        view, k = y // 2, y % 2
        start = (view // 2) * blocks * PACKET + DATA_ROWS + k
        rows = pl.ds(start, blocks, stride=PACKET)
        same = (core == view % 2).astype(jnp.int32) > 0
        tiles.append(jnp.where(same, near[rows, :], far[rows, :]))
    est = jnp.concatenate(tiles, axis=0)

    lane, row = lane_ids(SIDE), row_ids(SIDE)
    lane_x, lane_y = lane & (SIDE - 1), lane >> 3
    signed = jnp.where(lane < LANES // 2, lane, lane - LANES)

    def kernel_row(meta, which, offset):
        inside = (offset >= -reach) & (offset <= reach)
        index = jnp.clip(offset, -reach, reach) + (which * width + reach)
        return jnp.where(inside, lane_pick(meta, index), 0.0)

    band = jnp.abs(lane_ids(LANES) - row_ids(LANES)) <= reach

    def toeplitz(base):
        rolled = pltpu.roll(jnp.tile(base, (LANES // SIDE, 1)), 0, 1, stride=1, stride_axis=0)
        return jnp.where(band, rolled, 0.0)

    forward_side, forward_depth, back_side, back_depth = [], [], [], []
    metas = []
    for ref, start in sources:
        at = start + DATA_ROWS + 2
        meta = jnp.broadcast_to(ref[at : at + 1, :], (SIDE, LANES))
        metas.append(meta)
        forward_depth.append(right(toeplitz(kernel_row(meta, 2, -signed))))
    forward_depth = jnp.concatenate(forward_depth, axis=1)
    for meta in metas:
        for sign, sides in ((1, forward_side), (-1, back_side)):
            x_tile = kernel_row(meta, 0, sign * (lane_x - row))
            y_tile = kernel_row(meta, 1, sign * (lane_y - row))
            side = jnp.concatenate([x_tile * y_tile[y : y + 1, :] for y in range(SIDE)], axis=0)
            sides.append(left(side[:, : SIDE * SIDE]))
    recorded = []
    for ref, start in sources:
        labels = ref[pl.ds(start + DATA_ROWS + 2, blocks, stride=PACKET), :]
        slabs = [jnp.zeros((SIDE, LANES), jnp.float32)] * SIDE
        for s in range(2):
            spread = lane_pick(labels, jnp.full((SIDE, LANES), 3 * width + s, jnp.int32))
            for b in range(blocks):
                at = start + b * PACKET + s * SIDE
                label = jnp.broadcast_to(spread[b : b + 1, :], (SIDE, LANES))
                slab = ref[at : at + SIDE, :]
                for y in range(SIDE):
                    slabs[y] = jnp.where(label == y, slab, slabs[y])
        recorded.append(jnp.concatenate(slabs, axis=0))
    for meta in metas:
        back_depth.append(right(toeplitz(kernel_row(meta, 2, signed))))

    for step in range(ITERS):
        deep = matmul(left(est), forward_depth)
        deep = [right(deep[:, v * LANES : (v + 1) * LANES]) for v in views]
        blurred = [matmul(forward_side[v], deep[v]) for v in views]
        ratios = [right(recorded[v] / blurred[v]) for v in views]
        spread = [left(matmul(back_side[v], ratios[v])) for v in views]
        corr = [matmul(spread[v], back_depth[v]) for v in views]
        roots = [lax.rsqrt(corr[v] * corr[v + 1]) for v in views[::2]]
        est = est * lax.rsqrt(roots[0] * roots[1])
    held[...] = est
    out[...] = held[pl.ds(block, SIDE, stride=SIDE), :]


def on_device_small(estimate, view_data, taps_x, taps_y, taps_z, owner):
    blocks = lax.axis_size("block")
    views = lax.axis_size("view")
    reach = taps_x.shape[1] // 2
    groups = views // 2
    copies = groups * blocks
    smem = pl.BlockSpec(memory_space=pltpu.SMEM)
    vmem = pl.BlockSpec(memory_space=pltpu.VMEM)
    packet = pl.pallas_call(
        functools.partial(pack_kernel, copies),
        out_shape=pltpu.VMEM((copies, PACKET, LANES), jnp.float32),
        in_specs=[smem] + [vmem] * 5,
        out_specs=vmem,
        scratch_shapes=[pltpu.VMEM((1, LANES), jnp.float32)],
        name="pack",
    )(owner.reshape(-1), estimate.reshape(SIDE, LANES), view_data.reshape(DATA_ROWS, LANES), taps_x, taps_y, taps_z)
    alike = [[(2 * g + c) * blocks + b for g in range(groups) for b in range(blocks)] for c in range(2)]
    near = lax.all_to_all(packet, ("view", "block"), 0, 0, axis_index_groups=alike, tiled=True)
    near = near.reshape(copies * PACKET, LANES)
    far = lax.ppermute(near, "view", [(v, v ^ 1) for v in range(views)])
    near = pltpu.with_memory_space_constraint(near, pltpu.VMEM)
    far = pltpu.with_memory_space_constraint(far, pltpu.VMEM)
    joined = pl.pallas_call(
        functools.partial(volume_kernel, blocks, groups, reach),
        out_shape=jax.ShapeDtypeStruct((SIDE, LANES), jnp.float32),
        in_specs=[vmem] * 2,
        out_specs=vmem,
        scratch_shapes=[pltpu.VMEM((SIDE * SIDE, LANES), jnp.float32)],
        name="volume",
    )(near, far)
    return joined.reshape(estimate.shape)


def fits_one_device(estimate, view_data, taps_x, blocks, views):
    thin, total_y, depth = estimate.shape
    return (
        (thin, blocks, total_y, depth) == (1, SIDE, SIDE, LANES)
        and view_data.shape[1] == 2
        and views == 4
        and taps_x.shape[1] % 2 == 1
        and 3 * taps_x.shape[1] + 2 <= LANES
    )


def band_matrix(taps, length):
    width = taps.shape[0]
    reach = width // 2
    rows = jnp.arange(length, dtype=jnp.int32)[:, None]
    cols = jnp.arange(length, dtype=jnp.int32)[None, :]
    offset = cols - rows + reach
    inside = (offset >= 0) & (offset < width)
    index = jnp.clip(offset, 0, width - 1)
    values = jnp.take(taps, index.reshape(-1), axis=0).reshape(length, length)
    return jnp.where(inside, values, jnp.zeros_like(values))


def on_device(estimate, view_data, taps_x, taps_y, taps_z, owner):
    blocks = lax.axis_size("block")
    views = lax.axis_size("view")
    if fits_one_device(estimate, view_data, taps_x, blocks, views):
        return on_device_small(estimate, view_data, taps_x, taps_y, taps_z, owner)
    thin = estimate.shape[0]
    total_y = estimate.shape[1]
    depth = estimate.shape[2]
    total_x = thin * blocks
    slots = view_data.shape[1]
    own = owner[0, :, 0]
    order = jnp.arange(blocks, dtype=jnp.int32)
    earlier = (own[:, None] == own[None, :]) & (order[None, :] < order[:, None])
    place = jnp.sum(earlier.astype(jnp.int32), axis=1)
    slot_ids = jnp.arange(slots, dtype=jnp.int32)
    hits = (place[None, None, :] == slot_ids[:, None, None]) & (
        own[None, None, :] == order[None, :, None]
    )
    filled = jnp.any(hits, axis=2).astype(jnp.float32)
    source_slab = jnp.sum(jnp.where(hits, order[None, None, :], 0), axis=2)
    return_index = place * blocks + own
    device = lax.axis_index("block")
    held = jnp.sum((own == device).astype(jnp.int32))
    live = (slot_ids < held)[:, None, None, None]
    m_x = band_matrix(taps_x[0], total_x)
    m_y = band_matrix(taps_y[0], total_y)
    m_z = band_matrix(taps_z[0], depth)
    recorded = view_data[0]
    est = estimate
    for step in range(ITERS):
        forward = jnp.einsum("ij,xjz->xiz", m_y, est, precision=HIGH)
        pieces = forward.reshape(thin, blocks, thin, depth)
        picked = jnp.take(pieces, source_slab.reshape(-1), axis=1)
        picked = picked.reshape(thin, slots, blocks, thin, depth).transpose(1, 2, 0, 3, 4)
        picked = picked * filled[:, :, None, None, None]
        arrived = lax.all_to_all(picked, "block", split_axis=1, concat_axis=1, tiled=True)
        held_est = arrived.reshape(slots, total_x, thin, depth)
        blurred = jnp.einsum("ij,sjyz->siyz", m_x, held_est, precision=HIGH)
        blurred = jnp.einsum("sxyj,ij->sxyi", blurred, m_z, precision=HIGH)
        ratio = jnp.where(live, recorded / jnp.where(live, blurred, 1.0), 0.0)
        back = jnp.einsum("ji,sjyz->siyz", m_x, ratio, precision=HIGH)
        back = jnp.einsum("sxyj,ji->sxyi", back, m_z, precision=HIGH)
        returned = lax.all_to_all(
            back.reshape(slots, blocks, thin, thin, depth),
            "block",
            split_axis=1,
            concat_axis=1,
            tiled=True,
        )
        flat = returned.reshape(slots * blocks, thin, thin, depth)
        gathered = jnp.take(flat, return_index, axis=0)
        corr = gathered.transpose(1, 0, 2, 3).reshape(thin, total_y, depth)
        corr = jnp.einsum("ji,xjz->xiz", m_y, corr, precision=HIGH)
        logs = lax.psum(jnp.log(corr), "view")
        est = est * jnp.exp(logs / views)
    return est


def solution(mesh):
    in_specs = (
        P("block", None, None),
        P("view", "block", None, None, None),
        P("view", None),
        P("view", None),
        P("view", None),
        P("view", None, None),
    )
    out_specs = P("block", None, None)
    return jax.shard_map(
        on_device, mesh=mesh, in_specs=in_specs, out_specs=out_specs, check_vma=False
    )
```

```python
import functools

import jax
import jax.numpy as jnp
from jax import lax
from jax.experimental import pallas as pl
from jax.experimental.pallas import tpu as pltpu
from jax.sharding import PartitionSpec as P

ITERS = 2

HIGH = lax.Precision.HIGHEST

SIDE = 8
LANES = 128
DATA_ROWS = 16
PACKET = 24
FIRST = 5


def lane_ids(rows):
    return lax.broadcasted_iota(jnp.int32, (rows, LANES), 1)


def row_ids(rows):
    return lax.broadcasted_iota(jnp.int32, (rows, LANES), 0)


def pack_kernel(copies, own, est, data, tx, ty, tz, out, meta):
    block = lax.axis_index("block")
    view = lax.axis_index("view")
    width = tx.shape[1]
    first = jnp.int32(-1)
    second = jnp.int32(-1)
    for y in range(SIDE):
        mine = own[y] == block
        second = jnp.where(mine & (first >= 0), y, second)
        first = jnp.where(mine & (first < 0), y, first)
    lane = lane_ids(1)
    meta[...] = jnp.where(lane == 3 * width, first, second).astype(jnp.float32)
    for k, taps in enumerate((tx, ty, tz)):
        meta[:, k * width : (k + 1) * width] = taps[...]
    row = row_ids(SIDE)
    tile = jnp.broadcast_to(meta[...], (SIDE, LANES))
    for k in range(2):
        tile = jnp.where(row == k, est[pl.ds(2 * view + k, 1), :], tile)
    lower, upper = data[:SIDE], data[SIDE:]
    for k in range(copies):
        out[k, :SIDE] = lower
        out[k, SIDE:DATA_ROWS] = upper
        out[k, DATA_ROWS:] = tile


def halves(value):
    high = value.astype(jnp.bfloat16)
    low = (value - high.astype(jnp.float32)).astype(jnp.bfloat16)
    return high, low


def matmul(a, b):
    return jnp.dot(a, b, preferred_element_type=jnp.float32)


def left(value):
    high, low = halves(value)
    return jnp.concatenate([high, low, high], axis=1)


def right(value):
    high, low = halves(value)
    return jnp.concatenate([high, high, low], axis=0)


def lane_pick(tile, index):
    return jnp.take_along_axis(tile, index, axis=1)


def volume_kernel(blocks, groups, reach, near, far, out, held):
    block = lax.axis_index("block")
    core = lax.axis_index("view") & 1
    width = 2 * reach + 1
    sources = [(ref, g * blocks * PACKET) for ref in (near, far) for g in range(groups)]
    views = range(len(sources))

    tiles = []
    for y in range(SIDE):
        view, k = y // 2, y % 2
        start = (groups - 1 - view // 2) * blocks * PACKET + DATA_ROWS + k
        rows = pl.ds(start, blocks, stride=PACKET)
        same = (core == view % 2).astype(jnp.int32) > 0
        tiles.append(jnp.where(same, near[rows, :], far[rows, :]))
    est = jnp.concatenate(tiles, axis=0)

    lane, row = lane_ids(SIDE), row_ids(SIDE)
    lane_x, lane_y = lane & (SIDE - 1), lane >> 3
    turned = lambda j: (j + FIRST) & (SIDE - 1)
    signed = jnp.where(lane < LANES // 2, lane, lane - LANES)

    def kernel_row(meta, which, offset):
        inside = (offset >= -reach) & (offset <= reach)
        index = jnp.clip(offset, -reach, reach) + (which * width + reach)
        return jnp.where(inside, lane_pick(meta, index), 0.0)

    band = jnp.abs(lane_ids(LANES) - row_ids(LANES)) <= reach

    def toeplitz(base):
        rolled = pltpu.roll(jnp.tile(base, (LANES // SIDE, 1)), 0, 1, stride=1, stride_axis=0)
        return jnp.where(band, rolled, 0.0)

    forward_side, forward_depth, back_side, back_depth = [], [], [], []
    metas = []
    for ref, start in sources:
        at = start + DATA_ROWS + 2
        meta = jnp.broadcast_to(ref[at : at + 1, :], (SIDE, LANES))
        metas.append(meta)
        forward_depth.append(right(toeplitz(kernel_row(meta, 2, -signed))))
    forward_depth = jnp.concatenate(forward_depth, axis=1)
    for meta in metas:
        forward = (turned(lane_x) - row, lane_y - row, forward_side)
        back = (turned(row) - lane_x, row - lane_y, back_side)
        for x_offset, y_offset, sides in (forward, back):
            x_tile = kernel_row(meta, 0, x_offset)
            y_tile = kernel_row(meta, 1, y_offset)
            side = jnp.concatenate([x_tile * y_tile[y : y + 1, :] for y in range(SIDE)], axis=0)
            sides.append(left(side[:, : SIDE * SIDE]))
    recorded = []
    for ref, start in sources:
        labels = ref[pl.ds(start + DATA_ROWS + 2, blocks, stride=PACKET), :]
        slabs = [jnp.zeros((SIDE, LANES), jnp.float32)] * SIDE
        for s in range(2):
            spread = lane_pick(labels, jnp.full((SIDE, LANES), 3 * width + s, jnp.int32))
            for b in range(blocks):
                at = start + b * PACKET + s * SIDE
                label = jnp.broadcast_to(spread[b : b + 1, :], (SIDE, LANES))
                slab = ref[at : at + SIDE, :]
                for y in range(SIDE):
                    slabs[y] = jnp.where(label == y, slab, slabs[y])
        recorded.append(jnp.concatenate(slabs, axis=0))
    for meta in metas:
        back_depth.append(right(toeplitz(kernel_row(meta, 2, signed))))

    for step in range(ITERS):
        deep = matmul(left(est), forward_depth)
        deep = [right(deep[:, v * LANES : (v + 1) * LANES]) for v in views]
        blurred = [matmul(forward_side[v], deep[v]) for v in views]
        ratios = [right(recorded[v] / blurred[v]) for v in views]
        spread = [left(matmul(back_side[v], ratios[v])) for v in views]
        corr = [matmul(spread[v], back_depth[v]) for v in views]
        roots = [lax.rsqrt(corr[v] * corr[v + 1]) for v in views[::2]]
        est = est * lax.rsqrt(roots[0] * roots[1])
    held[...] = est
    out[...] = held[pl.ds((block - FIRST) & (SIDE - 1), SIDE, stride=SIDE), :]


def on_device_small(estimate, view_data, taps_x, taps_y, taps_z, owner):
    blocks = lax.axis_size("block")
    views = lax.axis_size("view")
    reach = taps_x.shape[1] // 2
    groups = views // 2
    copies = groups * blocks
    smem = pl.BlockSpec(memory_space=pltpu.SMEM)
    vmem = pl.BlockSpec(memory_space=pltpu.VMEM)
    packet = pl.pallas_call(
        functools.partial(pack_kernel, copies),
        out_shape=pltpu.VMEM((copies, PACKET, LANES), jnp.float32),
        in_specs=[smem] + [vmem] * 5,
        out_specs=vmem,
        scratch_shapes=[pltpu.VMEM((1, LANES), jnp.float32)],
        name="pack",
    )(owner.reshape(-1), estimate.reshape(SIDE, LANES), view_data.reshape(DATA_ROWS, LANES), taps_x, taps_y, taps_z)
    ring = [(FIRST + j) % blocks for j in range(blocks)]
    alike = [[(2 * g + c) * blocks + b for g in reversed(range(groups)) for b in ring] for c in range(2)]
    near = lax.all_to_all(packet, ("view", "block"), 0, 0, axis_index_groups=alike, tiled=True)
    near = near.reshape(copies * PACKET, LANES)
    far = lax.ppermute(near, "view", [(v, v ^ 1) for v in range(views)])
    near = pltpu.with_memory_space_constraint(near, pltpu.VMEM)
    far = pltpu.with_memory_space_constraint(far, pltpu.VMEM)
    joined = pl.pallas_call(
        functools.partial(volume_kernel, blocks, groups, reach),
        out_shape=jax.ShapeDtypeStruct((SIDE, LANES), jnp.float32),
        in_specs=[vmem] * 2,
        out_specs=vmem,
        scratch_shapes=[pltpu.VMEM((SIDE * SIDE, LANES), jnp.float32)],
        name="volume",
    )(near, far)
    return joined.reshape(estimate.shape)


def fits_one_device(estimate, view_data, taps_x, blocks, views):
    thin, total_y, depth = estimate.shape
    return (
        (thin, blocks, total_y, depth) == (1, SIDE, SIDE, LANES)
        and view_data.shape[1] == 2
        and views == 4
        and taps_x.shape[1] % 2 == 1
        and 3 * taps_x.shape[1] + 2 <= LANES
    )


def band_matrix(taps, length):
    width = taps.shape[0]
    reach = width // 2
    rows = jnp.arange(length, dtype=jnp.int32)[:, None]
    cols = jnp.arange(length, dtype=jnp.int32)[None, :]
    offset = cols - rows + reach
    inside = (offset >= 0) & (offset < width)
    index = jnp.clip(offset, 0, width - 1)
    values = jnp.take(taps, index.reshape(-1), axis=0).reshape(length, length)
    return jnp.where(inside, values, jnp.zeros_like(values))


def on_device(estimate, view_data, taps_x, taps_y, taps_z, owner):
    blocks = lax.axis_size("block")
    views = lax.axis_size("view")
    if fits_one_device(estimate, view_data, taps_x, blocks, views):
        return on_device_small(estimate, view_data, taps_x, taps_y, taps_z, owner)
    thin = estimate.shape[0]
    total_y = estimate.shape[1]
    depth = estimate.shape[2]
    total_x = thin * blocks
    slots = view_data.shape[1]
    own = owner[0, :, 0]
    order = jnp.arange(blocks, dtype=jnp.int32)
    earlier = (own[:, None] == own[None, :]) & (order[None, :] < order[:, None])
    place = jnp.sum(earlier.astype(jnp.int32), axis=1)
    slot_ids = jnp.arange(slots, dtype=jnp.int32)
    hits = (place[None, None, :] == slot_ids[:, None, None]) & (
        own[None, None, :] == order[None, :, None]
    )
    filled = jnp.any(hits, axis=2).astype(jnp.float32)
    source_slab = jnp.sum(jnp.where(hits, order[None, None, :], 0), axis=2)
    return_index = place * blocks + own
    device = lax.axis_index("block")
    held = jnp.sum((own == device).astype(jnp.int32))
    live = (slot_ids < held)[:, None, None, None]
    m_x = band_matrix(taps_x[0], total_x)
    m_y = band_matrix(taps_y[0], total_y)
    m_z = band_matrix(taps_z[0], depth)
    recorded = view_data[0]
    est = estimate
    for step in range(ITERS):
        forward = jnp.einsum("ij,xjz->xiz", m_y, est, precision=HIGH)
        pieces = forward.reshape(thin, blocks, thin, depth)
        picked = jnp.take(pieces, source_slab.reshape(-1), axis=1)
        picked = picked.reshape(thin, slots, blocks, thin, depth).transpose(1, 2, 0, 3, 4)
        picked = picked * filled[:, :, None, None, None]
        arrived = lax.all_to_all(picked, "block", split_axis=1, concat_axis=1, tiled=True)
        held_est = arrived.reshape(slots, total_x, thin, depth)
        blurred = jnp.einsum("ij,sjyz->siyz", m_x, held_est, precision=HIGH)
        blurred = jnp.einsum("sxyj,ij->sxyi", blurred, m_z, precision=HIGH)
        ratio = jnp.where(live, recorded / jnp.where(live, blurred, 1.0), 0.0)
        back = jnp.einsum("ji,sjyz->siyz", m_x, ratio, precision=HIGH)
        back = jnp.einsum("sxyj,ji->sxyi", back, m_z, precision=HIGH)
        returned = lax.all_to_all(
            back.reshape(slots, blocks, thin, thin, depth),
            "block",
            split_axis=1,
            concat_axis=1,
            tiled=True,
        )
        flat = returned.reshape(slots * blocks, thin, thin, depth)
        gathered = jnp.take(flat, return_index, axis=0)
        corr = gathered.transpose(1, 0, 2, 3).reshape(thin, total_y, depth)
        corr = jnp.einsum("ji,xjz->xiz", m_y, corr, precision=HIGH)
        logs = lax.psum(jnp.log(corr), "view")
        est = est * jnp.exp(logs / views)
    return est


def solution(mesh):
    in_specs = (
        P("block", None, None),
        P("view", "block", None, None, None),
        P("view", None),
        P("view", None),
        P("view", None),
        P("view", None, None),
    )
    out_specs = P("block", None, None)
    return jax.shard_map(
        on_device, mesh=mesh, in_specs=in_specs, out_specs=out_specs, check_vma=False
    )
```

```python
import functools

import jax
import jax.numpy as jnp
from jax import lax
from jax.experimental import pallas as pl
from jax.experimental.pallas import tpu as pltpu
from jax.sharding import PartitionSpec as P

ITERS = 2

HIGH = lax.Precision.HIGHEST

SIDE = 8
LANES = 128
DATA_ROWS = 16
EST_ROWS = 4
META = DATA_ROWS + EST_ROWS
PACKET = META + 1
FIRST = 5


def turned(j):
    return (j + FIRST) & (SIDE - 1)


def late(j):
    return int(turned(j) >= SIDE // 2)


def lane_ids(rows):
    return lax.broadcasted_iota(jnp.int32, (rows, LANES), 1)


def row_ids(rows):
    return lax.broadcasted_iota(jnp.int32, (rows, LANES), 0)


def pack_kernel(copies, own, est, data, tx, ty, tz, out, meta):
    block = lax.axis_index("block")
    group = lax.axis_index("view") >> 1
    width = tx.shape[1]
    first = jnp.int32(-1)
    second = jnp.int32(-1)
    for y in range(SIDE):
        mine = own[y] == block
        second = jnp.where(mine & (first >= 0), y, second)
        first = jnp.where(mine & (first < 0), y, first)
    meta[...] = jnp.where(lane_ids(1) == 3 * width, first, second).astype(jnp.float32)
    for k, taps in enumerate((tx, ty, tz)):
        meta[:, k * width : (k + 1) * width] = taps[...]
    row = meta[...]
    share = jnp.where(group == 0, est[:EST_ROWS, :], est[EST_ROWS:, :])
    lower, upper = data[:SIDE], data[SIDE:]
    for k in range(copies):
        at = k * PACKET
        out[at : at + SIDE, :] = lower
        out[at + SIDE : at + DATA_ROWS, :] = upper
        out[at + DATA_ROWS : at + META, :] = share
        out[at + META : at + PACKET, :] = row


def halves(value):
    high = value.astype(jnp.bfloat16)
    low = (value - high.astype(jnp.float32)).astype(jnp.bfloat16)
    return high, low


def matmul(a, b):
    return jnp.dot(a, b, preferred_element_type=jnp.float32)


def left(value):
    high, low = halves(value)
    return jnp.concatenate([high, low, high], axis=1)


def right(value):
    high, low = halves(value)
    return jnp.concatenate([high, high, low], axis=0)


def lane_pick(tile, index):
    return jnp.take_along_axis(tile, index, axis=1)


def placed(slabs, ref, groups, width, flip):
    for g in range(groups):
        start = g * SIDE * PACKET
        labels = ref[pl.ds(start + META, SIDE, stride=PACKET), :]
        for s in range(2):
            spread = lane_pick(labels, jnp.full((SIDE, LANES), 3 * width + s, jnp.int32))
            for j in range(SIDE):
                at = start + j * PACKET + s * SIDE
                label = jnp.broadcast_to(spread[j : j + 1, :], (SIDE, LANES))
                slab = ref[at : at + SIDE, :]
                mine = slabs[(late(j) ^ flip) * groups + g]
                for y in range(SIDE):
                    mine[y] = jnp.where(label == y, slab, mine[y])


def blur(est, forward_depth, forward_side, views):
    deep = matmul(left(est), forward_depth)
    deep = [right(deep[:, v * LANES : (v + 1) * LANES]) for v in views]
    return [matmul(forward_side[v], deep[v]) for v in views]


def prepare_kernel(groups, reach, near, est_out, inverse, slabs_out, forward_depth, forward_side, back_side, back_depth):
    width = 2 * reach + 1
    views = range(2 * groups)
    tiles = []
    for y in range(SIDE):
        start = (groups - 1 - y // EST_ROWS) * SIDE * PACKET + DATA_ROWS + y % EST_ROWS
        tiles.append(near[pl.ds(start, SIDE, stride=PACKET), :])
    est = jnp.concatenate(tiles, axis=0)
    est_out[...] = est

    lane, row = lane_ids(SIDE), row_ids(SIDE)
    lane_x, lane_y = lane & (SIDE - 1), lane >> 3
    signed = jnp.where(lane < LANES // 2, lane, lane - LANES)

    def kernel_row(meta, which, offset):
        inside = (offset >= -reach) & (offset <= reach)
        index = jnp.clip(offset, -reach, reach) + (which * width + reach)
        return jnp.where(inside, lane_pick(meta, index), 0.0)

    band = jnp.abs(lane_ids(LANES) - row_ids(LANES)) <= reach

    def toeplitz(base):
        rolled = pltpu.roll(jnp.tile(base, (LANES // SIDE, 1)), 0, 1, stride=1, stride_axis=0)
        return jnp.where(band, rolled, 0.0)

    metas = []
    for v in views:
        j = [late(j) for j in range(SIDE)].index(v // groups)
        at = ((v % groups) * SIDE + j) * PACKET + META
        metas.append(jnp.broadcast_to(near[at : at + 1, :], (SIDE, LANES)))
    forward = [right(toeplitz(kernel_row(meta, 2, -signed))) for meta in metas]
    sides = []
    for v, meta in enumerate(metas):
        for x_offset, y_offset, out in (
            (turned(lane_x) - row, lane_y - row, forward_side),
            (turned(row) - lane_x, row - lane_y, back_side),
        ):
            x_tile = kernel_row(meta, 0, x_offset)
            y_tile = kernel_row(meta, 1, y_offset)
            side = jnp.concatenate([x_tile * y_tile[y : y + 1, :] for y in range(SIDE)], axis=0)
            side = left(side[:, : SIDE * SIDE])
            out[v] = side
            if out is forward_side:
                sides.append(side)
    forward = jnp.concatenate(forward, axis=1)
    forward_depth[...] = forward
    blurred = blur(est, forward, sides, views)
    slabs = [[jnp.zeros((SIDE, LANES), jnp.float32)] * SIDE for _ in views]
    placed(slabs, near, groups, width, 0)
    for v, meta in enumerate(metas):
        back_depth[:, v * LANES : (v + 1) * LANES] = right(toeplitz(kernel_row(meta, 2, signed)))
        slabs_out[v] = jnp.concatenate(slabs[v], axis=0)
        inverse[v] = 1.0 / blurred[v]


def finish_kernel(groups, width, far, est_in, inverse, slabs_in, forward_depth, forward_side, back_side, back_depth, out, held):
    block = lax.axis_index("block")
    views = range(2 * groups)
    slabs = [[slabs_in[v, y * SIDE : (y + 1) * SIDE, :] for y in range(SIDE)] for v in views]
    placed(slabs, far, groups, width, 1)
    recorded = [jnp.concatenate(slabs[v], axis=0) for v in views]
    est = est_in[...]
    for step in range(ITERS):
        if step == 0:
            ratios = [recorded[v] * inverse[v] for v in views]
        else:
            blurred = blur(est, forward_depth[...], [forward_side[v] for v in views], views)
            ratios = [recorded[v] / blurred[v] for v in views]
        ratios = [right(ratios[v]) for v in views]
        spread = [left(matmul(back_side[v], ratios[v])) for v in views]
        corr = [matmul(spread[v], back_depth[:, v * LANES : (v + 1) * LANES]) for v in views]
        roots = [lax.rsqrt(corr[v] * corr[v + 1]) for v in views[::2]]
        est = est * lax.rsqrt(roots[0] * roots[1])
    held[...] = est
    out[...] = held[pl.ds((block - FIRST) & (SIDE - 1), SIDE, stride=SIDE), :]


def in_vmem(value):
    return pltpu.with_memory_space_constraint(value, pltpu.VMEM)


def on_device_small(estimate, view_data, taps_x, taps_y, taps_z, owner):
    blocks = lax.axis_size("block")
    views = lax.axis_size("view")
    width = taps_x.shape[1]
    groups = views // 2
    copies = groups * blocks
    smem = pl.BlockSpec(memory_space=pltpu.SMEM)
    vmem = pl.BlockSpec(memory_space=pltpu.VMEM)
    packet = pl.pallas_call(
        functools.partial(pack_kernel, copies),
        out_shape=pltpu.VMEM((copies * PACKET, LANES), jnp.float32),
        in_specs=[smem] + [vmem] * 5,
        out_specs=vmem,
        scratch_shapes=[pltpu.VMEM((1, LANES), jnp.float32)],
        name="pack",
    )(owner.reshape(-1), estimate.reshape(SIDE, LANES), view_data.reshape(DATA_ROWS, LANES), taps_x, taps_y, taps_z)
    alike = [
        [(2 * g + (k ^ late(j))) * blocks + turned(j) for g in reversed(range(groups)) for j in range(blocks)]
        for k in range(2)
    ]
    near = lax.all_to_all(
        packet.reshape(copies, PACKET, 1, LANES), ("view", "block"), 0, 0, axis_index_groups=alike, tiled=True
    )
    near = near.reshape(copies * PACKET, LANES)
    far = lax.ppermute(near, "view", [(v, v ^ 1) for v in range(views)])
    wide = jnp.bfloat16
    prepared = pl.pallas_call(
        functools.partial(prepare_kernel, groups, width // 2),
        out_shape=[
            pltpu.VMEM((SIDE * SIDE, LANES), jnp.float32),
            pltpu.VMEM((views, SIDE * SIDE, LANES), jnp.float32),
            pltpu.VMEM((views, SIDE * SIDE, LANES), jnp.float32),
            pltpu.VMEM((3 * LANES, views * LANES), wide),
            pltpu.VMEM((views, SIDE * SIDE, 3 * SIDE * SIDE), wide),
            pltpu.VMEM((views, SIDE * SIDE, 3 * SIDE * SIDE), wide),
            pltpu.VMEM((3 * LANES, views * LANES), wide),
        ],
        in_specs=[vmem],
        out_specs=[vmem] * 7,
        name="prepare",
    )(in_vmem(near))
    joined = pl.pallas_call(
        functools.partial(finish_kernel, groups, width),
        out_shape=jax.ShapeDtypeStruct((SIDE, LANES), jnp.float32),
        in_specs=[vmem] * 8,
        out_specs=vmem,
        scratch_shapes=[pltpu.VMEM((SIDE * SIDE, LANES), jnp.float32)],
        name="finish",
    )(in_vmem(far), *[in_vmem(value) for value in prepared])
    return joined.reshape(estimate.shape)


def fits_one_device(estimate, view_data, taps_x, blocks, views):
    thin, total_y, depth = estimate.shape
    return (
        (thin, blocks, total_y, depth) == (1, SIDE, SIDE, LANES)
        and view_data.shape[1] == 2
        and views == 4
        and taps_x.shape[1] % 2 == 1
        and 3 * taps_x.shape[1] + 2 <= LANES
    )


def band_matrix(taps, length):
    width = taps.shape[0]
    reach = width // 2
    rows = jnp.arange(length, dtype=jnp.int32)[:, None]
    cols = jnp.arange(length, dtype=jnp.int32)[None, :]
    offset = cols - rows + reach
    inside = (offset >= 0) & (offset < width)
    index = jnp.clip(offset, 0, width - 1)
    values = jnp.take(taps, index.reshape(-1), axis=0).reshape(length, length)
    return jnp.where(inside, values, jnp.zeros_like(values))


def on_device(estimate, view_data, taps_x, taps_y, taps_z, owner):
    blocks = lax.axis_size("block")
    views = lax.axis_size("view")
    if fits_one_device(estimate, view_data, taps_x, blocks, views):
        return on_device_small(estimate, view_data, taps_x, taps_y, taps_z, owner)
    thin = estimate.shape[0]
    total_y = estimate.shape[1]
    depth = estimate.shape[2]
    total_x = thin * blocks
    slots = view_data.shape[1]
    own = owner[0, :, 0]
    order = jnp.arange(blocks, dtype=jnp.int32)
    earlier = (own[:, None] == own[None, :]) & (order[None, :] < order[:, None])
    place = jnp.sum(earlier.astype(jnp.int32), axis=1)
    slot_ids = jnp.arange(slots, dtype=jnp.int32)
    hits = (place[None, None, :] == slot_ids[:, None, None]) & (
        own[None, None, :] == order[None, :, None]
    )
    filled = jnp.any(hits, axis=2).astype(jnp.float32)
    source_slab = jnp.sum(jnp.where(hits, order[None, None, :], 0), axis=2)
    return_index = place * blocks + own
    device = lax.axis_index("block")
    held = jnp.sum((own == device).astype(jnp.int32))
    live = (slot_ids < held)[:, None, None, None]
    m_x = band_matrix(taps_x[0], total_x)
    m_y = band_matrix(taps_y[0], total_y)
    m_z = band_matrix(taps_z[0], depth)
    recorded = view_data[0]
    est = estimate
    for step in range(ITERS):
        forward = jnp.einsum("ij,xjz->xiz", m_y, est, precision=HIGH)
        pieces = forward.reshape(thin, blocks, thin, depth)
        picked = jnp.take(pieces, source_slab.reshape(-1), axis=1)
        picked = picked.reshape(thin, slots, blocks, thin, depth).transpose(1, 2, 0, 3, 4)
        picked = picked * filled[:, :, None, None, None]
        arrived = lax.all_to_all(picked, "block", split_axis=1, concat_axis=1, tiled=True)
        held_est = arrived.reshape(slots, total_x, thin, depth)
        blurred = jnp.einsum("ij,sjyz->siyz", m_x, held_est, precision=HIGH)
        blurred = jnp.einsum("sxyj,ij->sxyi", blurred, m_z, precision=HIGH)
        ratio = jnp.where(live, recorded / jnp.where(live, blurred, 1.0), 0.0)
        back = jnp.einsum("ji,sjyz->siyz", m_x, ratio, precision=HIGH)
        back = jnp.einsum("sxyj,ji->sxyi", back, m_z, precision=HIGH)
        returned = lax.all_to_all(
            back.reshape(slots, blocks, thin, thin, depth),
            "block",
            split_axis=1,
            concat_axis=1,
            tiled=True,
        )
        flat = returned.reshape(slots * blocks, thin, thin, depth)
        gathered = jnp.take(flat, return_index, axis=0)
        corr = gathered.transpose(1, 0, 2, 3).reshape(thin, total_y, depth)
        corr = jnp.einsum("ji,xjz->xiz", m_y, corr, precision=HIGH)
        logs = lax.psum(jnp.log(corr), "view")
        est = est * jnp.exp(logs / views)
    return est


def solution(mesh):
    in_specs = (
        P("block", None, None),
        P("view", "block", None, None, None),
        P("view", None),
        P("view", None),
        P("view", None),
        P("view", None, None),
    )
    out_specs = P("block", None, None)
    return jax.shard_map(
        on_device, mesh=mesh, in_specs=in_specs, out_specs=out_specs, check_vma=False
    )
```

```python
import functools

import jax
import jax.numpy as jnp
from jax import lax
from jax.experimental import pallas as pl
from jax.experimental.pallas import tpu as pltpu
from jax.sharding import PartitionSpec as P

ITERS = 2

HIGH = lax.Precision.HIGHEST

SIDE = 8
LANES = 128
DATA_ROWS = 16
EST_ROWS = 4
META = DATA_ROWS + EST_ROWS
PACKET = META + 1
FIRST = 5
STEP = 3


def turned(j):
    return (STEP * j + FIRST) & (SIDE - 1)


def late(j):
    return int(turned(j) >= SIDE // 2)


def lane_ids(rows):
    return lax.broadcasted_iota(jnp.int32, (rows, LANES), 1)


def row_ids(rows):
    return lax.broadcasted_iota(jnp.int32, (rows, LANES), 0)


def pack_kernel(copies, own, est, data, tx, ty, tz, out, meta):
    group = lax.axis_index("view") >> 1
    width = tx.shape[1]
    lane = lane_ids(1)
    slots = jnp.zeros((1, LANES), jnp.int32)
    for y in range(SIDE):
        place = sum((own[c] == own[y]).astype(jnp.int32) for c in range(y))
        slots = jnp.where(lane == 3 * width + y, 2 * own[y] + place, slots)
    meta[...] = slots.astype(jnp.float32)
    for k, taps in enumerate((tx, ty, tz)):
        meta[:, k * width : (k + 1) * width] = taps[...]
    row = meta[...]
    share = jnp.where(group == 0, est[:EST_ROWS, :], est[EST_ROWS:, :])
    lower, upper = data[:SIDE], data[SIDE:]
    for k in range(copies):
        at = k * PACKET
        out[at : at + SIDE, :] = lower
        out[at + SIDE : at + DATA_ROWS, :] = upper
        out[at + DATA_ROWS : at + META, :] = share
        out[at + META : at + PACKET, :] = row


def halves(value):
    high = value.astype(jnp.bfloat16)
    low = (value - high.astype(jnp.float32)).astype(jnp.bfloat16)
    return high, low


def matmul(a, b):
    return jnp.dot(a, b, preferred_element_type=jnp.float32)


def left(value):
    high, low = halves(value)
    return jnp.concatenate([high, low, high], axis=1)


def right(value):
    high, low = halves(value)
    return jnp.concatenate([high, high, low], axis=0)


def lane_pick(tile, index):
    return jnp.take_along_axis(tile, index, axis=1)


def placed(slabs, ref, groups, slots, flip):
    for v in range(2 * groups):
        for j in [j for j in range(SIDE) if late(j) ^ flip == v // groups]:
            for s in range(2):
                at = ((v % groups) * SIDE + j) * PACKET + s * SIDE
                slab = ref[at : at + SIDE, :]
                for y in range(SIDE):
                    slabs[v][y] = jnp.where(slots[v][y] == 2 * turned(j) + s, slab, slabs[v][y])


def spread_rows(tile):
    return [jnp.broadcast_to(tile[y : y + 1, :], (SIDE, LANES)) for y in range(SIDE)]


def blur(est, forward_depth, forward_side, views):
    deep = matmul(left(est), forward_depth)
    deep = [right(deep[:, v * LANES : (v + 1) * LANES]) for v in views]
    return [matmul(forward_side[v], deep[v]) for v in views]


def prepare_kernel(
    groups, reach, near, est_out, inverse, slabs_out, slots_out, forward_depth, forward_side, back_side, own_side, back_depth
):
    width = 2 * reach + 1
    block = lax.axis_index("block")
    views = range(2 * groups)
    tiles = []
    for y in range(SIDE):
        start = (groups - 1 - y // EST_ROWS) * SIDE * PACKET + DATA_ROWS + y % EST_ROWS
        tiles.append(near[pl.ds(start, SIDE, stride=PACKET), :])
    est = jnp.concatenate(tiles, axis=0)
    est_out[...] = est

    lane, row = lane_ids(SIDE), row_ids(SIDE)
    lane_x, lane_y = lane & (SIDE - 1), lane >> 3
    signed = jnp.where(lane < LANES // 2, lane, lane - LANES)

    def kernel_row(meta, which, offset):
        inside = (offset >= -reach) & (offset <= reach)
        index = jnp.clip(offset, -reach, reach) + (which * width + reach)
        return jnp.where(inside, lane_pick(meta, index), 0.0)

    band = jnp.abs(lane_ids(LANES) - row_ids(LANES)) <= reach

    def toeplitz(base):
        rolled = pltpu.roll(jnp.tile(base, (LANES // SIDE, 1)), 0, 1, stride=1, stride_axis=0)
        return jnp.where(band, rolled, 0.0)

    metas = []
    for v in views:
        j = [late(j) for j in range(SIDE)].index(v // groups)
        at = ((v % groups) * SIDE + j) * PACKET + META
        metas.append(jnp.broadcast_to(near[at : at + 1, :], (SIDE, LANES)))
    depth = [kernel_row(meta, 2, -signed) for meta in metas]
    ahead = [
        (kernel_row(meta, 0, turned(lane_x) - row), kernel_row(meta, 1, lane_y - row)) for meta in metas
    ]
    slots = [lane_pick(meta, row + 3 * width) for meta in metas]
    depth_back = [kernel_row(meta, 2, signed) for meta in metas]
    back_y = [kernel_row(meta, 1, row - lane_y) for meta in metas]
    back_x = [kernel_row(meta, 0, turned(row) - lane_x) for meta in metas]
    own_x = [kernel_row(meta, 0, block - lane_x) for meta in metas]

    def side_matrix(x_tile, y_tile):
        side = jnp.concatenate([x_tile * y_row for y_row in spread_rows(y_tile)], axis=0)
        return left(side[:, : SIDE * SIDE])

    forward = jnp.concatenate([right(toeplitz(base)) for base in depth], axis=1)
    sides = [side_matrix(x_tile, y_tile) for x_tile, y_tile in ahead]
    blurred = blur(est, forward, sides, views)
    slots = [spread_rows(tile) for tile in slots]
    slabs = [[jnp.zeros((SIDE, LANES), jnp.float32)] * SIDE for _ in views]
    placed(slabs, near, groups, slots, 0)
    forward_depth[...] = forward
    for v in views:
        forward_side[v] = sides[v]
        back_side[v] = side_matrix(back_x[v], back_y[v])
        own = own_x[v] * back_y[v]
        own_side[v] = left(jnp.concatenate([own, own], axis=0)[:, : SIDE * SIDE])
        back_depth[:, v * LANES : (v + 1) * LANES] = right(toeplitz(depth_back[v]))
        slabs_out[v] = jnp.concatenate(slabs[v], axis=0)
        slots_out[v] = jnp.concatenate(slots[v], axis=0)
    for v in views:
        inverse[v] = 1.0 / blurred[v]


def finish_kernel(
    groups,
    far,
    est_in,
    inverse,
    slabs_in,
    slots_in,
    forward_depth,
    forward_side,
    back_side,
    own_side,
    back_depth,
    out,
    held,
):
    block = lax.axis_index("block")
    views = range(2 * groups)
    slabs = [[slabs_in[v, y * SIDE : (y + 1) * SIDE, :] for y in range(SIDE)] for v in views]
    slots = [[slots_in[v, y * SIDE : (y + 1) * SIDE, :] for y in range(SIDE)] for v in views]
    placed(slabs, far, groups, slots, 1)
    recorded = [jnp.concatenate(slabs[v], axis=0) for v in views]
    est = est_in[...]
    for step in range(ITERS):
        if step == 0:
            ratios = [recorded[v] * inverse[v] for v in views]
        else:
            blurred = blur(est, forward_depth[...], [forward_side[v] for v in views], views)
            ratios = [recorded[v] / blurred[v] for v in views]
        ratios = [right(ratios[v]) for v in views]
        last = step == ITERS - 1
        back = own_side if last else back_side
        spread = [left(matmul(back[v], ratios[v])) for v in views]
        corr = [matmul(spread[v], back_depth[:, v * LANES : (v + 1) * LANES]) for v in views]
        if last:
            corr = [value[:SIDE] for value in corr]
            held[...] = est
            est = held[pl.ds((STEP * (block - FIRST)) & (SIDE - 1), SIDE, stride=SIDE), :]
        roots = [lax.rsqrt(corr[v] * corr[v + 1]) for v in views[::2]]
        est = est * lax.rsqrt(roots[0] * roots[1])
    out[...] = est


def in_vmem(value):
    return pltpu.with_memory_space_constraint(value, pltpu.VMEM)


def on_device_small(estimate, view_data, taps_x, taps_y, taps_z, owner):
    blocks = lax.axis_size("block")
    views = lax.axis_size("view")
    width = taps_x.shape[1]
    groups = views // 2
    copies = groups * blocks
    smem = pl.BlockSpec(memory_space=pltpu.SMEM)
    vmem = pl.BlockSpec(memory_space=pltpu.VMEM)
    packet = pl.pallas_call(
        functools.partial(pack_kernel, copies),
        out_shape=pltpu.VMEM((copies * PACKET, LANES), jnp.float32),
        in_specs=[smem] + [vmem] * 5,
        out_specs=vmem,
        scratch_shapes=[pltpu.VMEM((1, LANES), jnp.float32)],
        name="pack",
    )(owner.reshape(-1), estimate.reshape(SIDE, LANES), view_data.reshape(DATA_ROWS, LANES), taps_x, taps_y, taps_z)
    alike = [
        [(2 * g + (k ^ late(j))) * blocks + turned(j) for g in reversed(range(groups)) for j in range(blocks)]
        for k in range(2)
    ]
    near = lax.all_to_all(
        packet.reshape(copies, PACKET, 1, LANES), ("view", "block"), 0, 0, axis_index_groups=alike, tiled=True
    )
    near = near.reshape(copies * PACKET, LANES)
    far = lax.ppermute(near, "view", [(v, v ^ 1) for v in range(views)])
    wide = jnp.bfloat16
    prepared = pl.pallas_call(
        functools.partial(prepare_kernel, groups, width // 2),
        out_shape=[
            pltpu.VMEM((SIDE * SIDE, LANES), jnp.float32),
            pltpu.VMEM((views, SIDE * SIDE, LANES), jnp.float32),
            pltpu.VMEM((views, SIDE * SIDE, LANES), jnp.float32),
            pltpu.VMEM((views, SIDE * SIDE, LANES), jnp.float32),
            pltpu.VMEM((3 * LANES, views * LANES), wide),
            pltpu.VMEM((views, SIDE * SIDE, 3 * SIDE * SIDE), wide),
            pltpu.VMEM((views, SIDE * SIDE, 3 * SIDE * SIDE), wide),
            pltpu.VMEM((views, 2 * SIDE, 3 * SIDE * SIDE), wide),
            pltpu.VMEM((3 * LANES, views * LANES), wide),
        ],
        in_specs=[vmem],
        out_specs=[vmem] * 9,
        name="prepare",
    )(in_vmem(near))
    joined = pl.pallas_call(
        functools.partial(finish_kernel, groups),
        out_shape=jax.ShapeDtypeStruct((SIDE, LANES), jnp.float32),
        in_specs=[vmem] * 10,
        out_specs=vmem,
        scratch_shapes=[pltpu.VMEM((SIDE * SIDE, LANES), jnp.float32)],
        name="finish",
    )(in_vmem(far), *[in_vmem(value) for value in prepared])
    return joined.reshape(estimate.shape)


def fits_one_device(estimate, view_data, taps_x, blocks, views):
    thin, total_y, depth = estimate.shape
    return (
        (thin, blocks, total_y, depth) == (1, SIDE, SIDE, LANES)
        and view_data.shape[1] == 2
        and views == 4
        and taps_x.shape[1] % 2 == 1
        and 3 * taps_x.shape[1] + SIDE <= LANES
    )


def band_matrix(taps, length):
    width = taps.shape[0]
    reach = width // 2
    rows = jnp.arange(length, dtype=jnp.int32)[:, None]
    cols = jnp.arange(length, dtype=jnp.int32)[None, :]
    offset = cols - rows + reach
    inside = (offset >= 0) & (offset < width)
    index = jnp.clip(offset, 0, width - 1)
    values = jnp.take(taps, index.reshape(-1), axis=0).reshape(length, length)
    return jnp.where(inside, values, jnp.zeros_like(values))


def on_device(estimate, view_data, taps_x, taps_y, taps_z, owner):
    blocks = lax.axis_size("block")
    views = lax.axis_size("view")
    if fits_one_device(estimate, view_data, taps_x, blocks, views):
        return on_device_small(estimate, view_data, taps_x, taps_y, taps_z, owner)
    thin = estimate.shape[0]
    total_y = estimate.shape[1]
    depth = estimate.shape[2]
    total_x = thin * blocks
    slots = view_data.shape[1]
    own = owner[0, :, 0]
    order = jnp.arange(blocks, dtype=jnp.int32)
    earlier = (own[:, None] == own[None, :]) & (order[None, :] < order[:, None])
    place = jnp.sum(earlier.astype(jnp.int32), axis=1)
    slot_ids = jnp.arange(slots, dtype=jnp.int32)
    hits = (place[None, None, :] == slot_ids[:, None, None]) & (
        own[None, None, :] == order[None, :, None]
    )
    filled = jnp.any(hits, axis=2).astype(jnp.float32)
    source_slab = jnp.sum(jnp.where(hits, order[None, None, :], 0), axis=2)
    return_index = place * blocks + own
    device = lax.axis_index("block")
    held = jnp.sum((own == device).astype(jnp.int32))
    live = (slot_ids < held)[:, None, None, None]
    m_x = band_matrix(taps_x[0], total_x)
    m_y = band_matrix(taps_y[0], total_y)
    m_z = band_matrix(taps_z[0], depth)
    recorded = view_data[0]
    est = estimate
    for step in range(ITERS):
        forward = jnp.einsum("ij,xjz->xiz", m_y, est, precision=HIGH)
        pieces = forward.reshape(thin, blocks, thin, depth)
        picked = jnp.take(pieces, source_slab.reshape(-1), axis=1)
        picked = picked.reshape(thin, slots, blocks, thin, depth).transpose(1, 2, 0, 3, 4)
        picked = picked * filled[:, :, None, None, None]
        arrived = lax.all_to_all(picked, "block", split_axis=1, concat_axis=1, tiled=True)
        held_est = arrived.reshape(slots, total_x, thin, depth)
        blurred = jnp.einsum("ij,sjyz->siyz", m_x, held_est, precision=HIGH)
        blurred = jnp.einsum("sxyj,ij->sxyi", blurred, m_z, precision=HIGH)
        ratio = jnp.where(live, recorded / jnp.where(live, blurred, 1.0), 0.0)
        back = jnp.einsum("ji,sjyz->siyz", m_x, ratio, precision=HIGH)
        back = jnp.einsum("sxyj,ji->sxyi", back, m_z, precision=HIGH)
        returned = lax.all_to_all(
            back.reshape(slots, blocks, thin, thin, depth),
            "block",
            split_axis=1,
            concat_axis=1,
            tiled=True,
        )
        flat = returned.reshape(slots * blocks, thin, thin, depth)
        gathered = jnp.take(flat, return_index, axis=0)
        corr = gathered.transpose(1, 0, 2, 3).reshape(thin, total_y, depth)
        corr = jnp.einsum("ji,xjz->xiz", m_y, corr, precision=HIGH)
        logs = lax.psum(jnp.log(corr), "view")
        est = est * jnp.exp(logs / views)
    return est


def solution(mesh):
    in_specs = (
        P("block", None, None),
        P("view", "block", None, None, None),
        P("view", None),
        P("view", None),
        P("view", None),
        P("view", None, None),
    )
    out_specs = P("block", None, None)
    return jax.shard_map(
        on_device, mesh=mesh, in_specs=in_specs, out_specs=out_specs, check_vma=False
    )
```

```python
import functools

import jax
import jax.numpy as jnp
from jax import lax
from jax.experimental import pallas as pl
from jax.experimental.pallas import tpu as pltpu
from jax.sharding import PartitionSpec as P

ITERS = 2

HIGH = lax.Precision.HIGHEST

SIDE = 8
LANES = 128
DATA_ROWS = 16
EST_ROWS = 4
META = DATA_ROWS + EST_ROWS
PACKET = META + 1
ORDER = (
    *((1, 5), (0, 2), (0, 1), (0, 6), (1, 1), (1, 2), (0, 4), (1, 4)),
    *((0, 5), (1, 0), (0, 7), (0, 0), (1, 3), (1, 6), (0, 3), (1, 7)),
)
LATE = {(g, b): int(b >= 4) for g, b in ORDER}


def lane_ids(rows):
    return lax.broadcasted_iota(jnp.int32, (rows, LANES), 1)


def row_ids(rows):
    return lax.broadcasted_iota(jnp.int32, (rows, LANES), 0)


def pack_kernel(copies, own, est, data, tx, ty, tz, out, meta):
    group = lax.axis_index("view") >> 1
    width = tx.shape[1]
    meta[...] = jnp.zeros_like(meta)
    meta[:, 3 * width : 3 * width + SIDE] = own[...].astype(jnp.float32)
    for k, taps in enumerate((tx, ty, tz)):
        meta[:, k * width : (k + 1) * width] = taps[...]
    row = meta[...]
    share = jnp.where(group == 0, est[:EST_ROWS, :], est[EST_ROWS:, :])
    lower, upper = data[:SIDE], data[SIDE:]
    for k in range(copies):
        at = k * PACKET
        out[at : at + SIDE, :] = lower
        out[at + SIDE : at + DATA_ROWS, :] = upper
        out[at + DATA_ROWS : at + META, :] = share
        out[at + META : at + PACKET, :] = row


def halves(value):
    high = value.astype(jnp.bfloat16)
    low = (value - high.astype(jnp.float32)).astype(jnp.bfloat16)
    return high, low


def matmul(a, b):
    return jnp.dot(a, b, preferred_element_type=jnp.float32)


def left(value):
    high, low = halves(value)
    return jnp.concatenate([high, low, high], axis=1)


def right(value):
    high, low = halves(value)
    return jnp.concatenate([high, high, low], axis=0)


def lane_pick(tile, index):
    return jnp.take_along_axis(tile, index, axis=1)


def placed(slabs, ref, groups, slots, flip):
    for p, (g, b) in enumerate(ORDER):
        v = (LATE[g, b] ^ flip) * groups + g
        for s in range(2):
            at = p * PACKET + s * SIDE
            slab = ref[at : at + SIDE, :]
            for y in range(SIDE):
                slabs[v][y] = jnp.where(slots[v][y] == 2 * b + s, slab, slabs[v][y])


def slot_numbers(owners):
    numbers = []
    for y, mine in enumerate(owners):
        place = jnp.zeros_like(mine)
        for other in owners[:y]:
            place += jnp.where(other == mine, 1.0, 0.0)
        numbers.append(2.0 * mine + place)
    return numbers


def spread_rows(tile):
    return [jnp.broadcast_to(tile[y : y + 1, :], (SIDE, LANES)) for y in range(SIDE)]


def blur(est, forward_depth, forward_side, views):
    deep = matmul(left(est), forward_depth)
    deep = [right(deep[:, v * LANES : (v + 1) * LANES]) for v in views]
    return [matmul(forward_side[v], deep[v]) for v in views]


def prepare_kernel(
    groups, reach, near, est_out, inverse, slabs_out, slots_out, forward_depth, forward_side, back_side, own_side, back_depth
):
    width = 2 * reach + 1
    block = lax.axis_index("block")
    views = range(2 * groups)
    for p, (g, b) in enumerate(ORDER):
        for i in range(EST_ROWS):
            y, at = g * EST_ROWS + i, p * PACKET + DATA_ROWS + i
            est_out[y * SIDE + b : y * SIDE + b + 1, :] = near[at : at + 1, :]
    est = est_out[...]

    lane, row = lane_ids(SIDE), row_ids(SIDE)
    lane_x, lane_y = lane & (SIDE - 1), lane >> 3
    signed = jnp.where(lane < LANES // 2, lane, lane - LANES)

    def kernel_row(meta, which, offset):
        inside = (offset >= -reach) & (offset <= reach)
        index = jnp.clip(offset, -reach, reach) + (which * width + reach)
        return jnp.where(inside, lane_pick(meta, index), 0.0)

    band = jnp.abs(lane_ids(LANES) - row_ids(LANES)) <= reach

    def toeplitz(base):
        rolled = pltpu.roll(jnp.tile(base, (LANES // SIDE, 1)), 0, 1, stride=1, stride_axis=0)
        return jnp.where(band, rolled, 0.0)

    metas = []
    for v in views:
        p = [(LATE[key], key[0]) for key in ORDER].index((v // groups, v % groups))
        at = p * PACKET + META
        metas.append(jnp.broadcast_to(near[at : at + 1, :], (SIDE, LANES)))
    depth = [kernel_row(meta, 2, -signed) for meta in metas]
    ahead = [
        (kernel_row(meta, 0, lane_x - row), kernel_row(meta, 1, lane_y - row)) for meta in metas
    ]
    owners = [lane_pick(meta, row + 3 * width) for meta in metas]
    depth_back = [kernel_row(meta, 2, signed) for meta in metas]
    back_y = [kernel_row(meta, 1, row - lane_y) for meta in metas]
    back_x = [kernel_row(meta, 0, row - lane_x) for meta in metas]
    own_x = [kernel_row(meta, 0, block - lane_x) for meta in metas]

    def side_matrix(x_tile, y_tile):
        side = jnp.concatenate([x_tile * y_row for y_row in spread_rows(y_tile)], axis=0)
        return left(side[:, : SIDE * SIDE])

    forward = jnp.concatenate([right(toeplitz(base)) for base in depth], axis=1)
    sides = [side_matrix(x_tile, y_tile) for x_tile, y_tile in ahead]
    blurred = blur(est, forward, sides, views)
    slots = [slot_numbers(spread_rows(tile)) for tile in owners]
    slabs = [[jnp.zeros((SIDE, LANES), jnp.float32)] * SIDE for _ in views]
    placed(slabs, near, groups, slots, 0)
    forward_depth[...] = forward
    for v in views:
        forward_side[v] = sides[v]
        back_side[v] = side_matrix(back_x[v], back_y[v])
        own = own_x[v] * back_y[v]
        own_side[v] = left(jnp.concatenate([own, own], axis=0)[:, : SIDE * SIDE])
        back_depth[:, v * LANES : (v + 1) * LANES] = right(toeplitz(depth_back[v]))
        slabs_out[v] = jnp.concatenate(slabs[v], axis=0)
        slots_out[v] = jnp.concatenate(slots[v], axis=0)
    for v in views:
        inverse[v] = 1.0 / blurred[v]


def finish_kernel(
    groups,
    far,
    est_in,
    inverse,
    slabs_in,
    slots_in,
    forward_depth,
    forward_side,
    back_side,
    own_side,
    back_depth,
    out,
    held,
):
    block = lax.axis_index("block")
    views = range(2 * groups)
    slabs = [[slabs_in[v, y * SIDE : (y + 1) * SIDE, :] for y in range(SIDE)] for v in views]
    slots = [[slots_in[v, y * SIDE : (y + 1) * SIDE, :] for y in range(SIDE)] for v in views]
    placed(slabs, far, groups, slots, 1)
    recorded = [jnp.concatenate(slabs[v], axis=0) for v in views]
    est = est_in[...]
    for step in range(ITERS):
        if step == 0:
            ratios = [recorded[v] * inverse[v] for v in views]
        else:
            blurred = blur(est, forward_depth[...], [forward_side[v] for v in views], views)
            ratios = [recorded[v] / blurred[v] for v in views]
        ratios = [right(ratios[v]) for v in views]
        last = step == ITERS - 1
        back = own_side if last else back_side
        spread = [left(matmul(back[v], ratios[v])) for v in views]
        corr = [matmul(spread[v], back_depth[:, v * LANES : (v + 1) * LANES]) for v in views]
        if last:
            corr = [value[:SIDE] for value in corr]
            held[...] = est
            est = held[pl.ds(block, SIDE, stride=SIDE), :]
        roots = [lax.rsqrt(corr[v] * corr[v + 1]) for v in views[::2]]
        est = est * lax.rsqrt(roots[0] * roots[1])
    out[...] = est


def in_vmem(value):
    return pltpu.with_memory_space_constraint(value, pltpu.VMEM)


def on_device_small(estimate, view_data, taps_x, taps_y, taps_z, owner):
    blocks = lax.axis_size("block")
    views = lax.axis_size("view")
    width = taps_x.shape[1]
    groups = views // 2
    copies = groups * blocks
    vmem = pl.BlockSpec(memory_space=pltpu.VMEM)
    packet = pl.pallas_call(
        functools.partial(pack_kernel, copies),
        out_shape=pltpu.VMEM((copies * PACKET, LANES), jnp.float32),
        in_specs=[vmem] * 6,
        out_specs=vmem,
        scratch_shapes=[pltpu.VMEM((1, LANES), jnp.float32)],
        name="pack",
    )(owner.reshape(1, SIDE), estimate.reshape(SIDE, LANES), view_data.reshape(DATA_ROWS, LANES), taps_x, taps_y, taps_z)
    alike = [[(2 * g + (k ^ LATE[g, b])) * blocks + b for g, b in ORDER] for k in range(2)]
    near = lax.all_to_all(
        packet.reshape(copies, PACKET, 1, LANES), ("view", "block"), 0, 0, axis_index_groups=alike, tiled=True
    )
    near = near.reshape(copies * PACKET, LANES)
    far = lax.ppermute(near, "view", [(v, v ^ 1) for v in range(views)])
    wide = jnp.bfloat16
    prepared = pl.pallas_call(
        functools.partial(prepare_kernel, groups, width // 2),
        out_shape=[
            pltpu.VMEM((SIDE * SIDE, LANES), jnp.float32),
            pltpu.VMEM((views, SIDE * SIDE, LANES), jnp.float32),
            pltpu.VMEM((views, SIDE * SIDE, LANES), jnp.float32),
            pltpu.VMEM((views, SIDE * SIDE, LANES), jnp.float32),
            pltpu.VMEM((3 * LANES, views * LANES), wide),
            pltpu.VMEM((views, SIDE * SIDE, 3 * SIDE * SIDE), wide),
            pltpu.VMEM((views, SIDE * SIDE, 3 * SIDE * SIDE), wide),
            pltpu.VMEM((views, 2 * SIDE, 3 * SIDE * SIDE), wide),
            pltpu.VMEM((3 * LANES, views * LANES), wide),
        ],
        in_specs=[vmem],
        out_specs=[vmem] * 9,
        name="prepare",
    )(in_vmem(near))
    joined = pl.pallas_call(
        functools.partial(finish_kernel, groups),
        out_shape=jax.ShapeDtypeStruct((SIDE, LANES), jnp.float32),
        in_specs=[vmem] * 10,
        out_specs=vmem,
        scratch_shapes=[pltpu.VMEM((SIDE * SIDE, LANES), jnp.float32)],
        name="finish",
    )(in_vmem(far), *[in_vmem(value) for value in prepared])
    return joined.reshape(estimate.shape)


def fits_one_device(estimate, view_data, taps_x, blocks, views):
    thin, total_y, depth = estimate.shape
    return (
        (thin, blocks, total_y, depth) == (1, SIDE, SIDE, LANES)
        and view_data.shape[1] == 2
        and views == 4
        and taps_x.shape[1] % 2 == 1
        and 3 * taps_x.shape[1] + SIDE <= LANES
    )


def band_matrix(taps, length):
    width = taps.shape[0]
    reach = width // 2
    rows = jnp.arange(length, dtype=jnp.int32)[:, None]
    cols = jnp.arange(length, dtype=jnp.int32)[None, :]
    offset = cols - rows + reach
    inside = (offset >= 0) & (offset < width)
    index = jnp.clip(offset, 0, width - 1)
    values = jnp.take(taps, index.reshape(-1), axis=0).reshape(length, length)
    return jnp.where(inside, values, jnp.zeros_like(values))


def on_device(estimate, view_data, taps_x, taps_y, taps_z, owner):
    blocks = lax.axis_size("block")
    views = lax.axis_size("view")
    if fits_one_device(estimate, view_data, taps_x, blocks, views):
        return on_device_small(estimate, view_data, taps_x, taps_y, taps_z, owner)
    thin = estimate.shape[0]
    total_y = estimate.shape[1]
    depth = estimate.shape[2]
    total_x = thin * blocks
    slots = view_data.shape[1]
    own = owner[0, :, 0]
    order = jnp.arange(blocks, dtype=jnp.int32)
    earlier = (own[:, None] == own[None, :]) & (order[None, :] < order[:, None])
    place = jnp.sum(earlier.astype(jnp.int32), axis=1)
    slot_ids = jnp.arange(slots, dtype=jnp.int32)
    hits = (place[None, None, :] == slot_ids[:, None, None]) & (
        own[None, None, :] == order[None, :, None]
    )
    filled = jnp.any(hits, axis=2).astype(jnp.float32)
    source_slab = jnp.sum(jnp.where(hits, order[None, None, :], 0), axis=2)
    return_index = place * blocks + own
    device = lax.axis_index("block")
    held = jnp.sum((own == device).astype(jnp.int32))
    live = (slot_ids < held)[:, None, None, None]
    m_x = band_matrix(taps_x[0], total_x)
    m_y = band_matrix(taps_y[0], total_y)
    m_z = band_matrix(taps_z[0], depth)
    recorded = view_data[0]
    est = estimate
    for step in range(ITERS):
        forward = jnp.einsum("ij,xjz->xiz", m_y, est, precision=HIGH)
        pieces = forward.reshape(thin, blocks, thin, depth)
        picked = jnp.take(pieces, source_slab.reshape(-1), axis=1)
        picked = picked.reshape(thin, slots, blocks, thin, depth).transpose(1, 2, 0, 3, 4)
        picked = picked * filled[:, :, None, None, None]
        arrived = lax.all_to_all(picked, "block", split_axis=1, concat_axis=1, tiled=True)
        held_est = arrived.reshape(slots, total_x, thin, depth)
        blurred = jnp.einsum("ij,sjyz->siyz", m_x, held_est, precision=HIGH)
        blurred = jnp.einsum("sxyj,ij->sxyi", blurred, m_z, precision=HIGH)
        ratio = jnp.where(live, recorded / jnp.where(live, blurred, 1.0), 0.0)
        back = jnp.einsum("ji,sjyz->siyz", m_x, ratio, precision=HIGH)
        back = jnp.einsum("sxyj,ji->sxyi", back, m_z, precision=HIGH)
        returned = lax.all_to_all(
            back.reshape(slots, blocks, thin, thin, depth),
            "block",
            split_axis=1,
            concat_axis=1,
            tiled=True,
        )
        flat = returned.reshape(slots * blocks, thin, thin, depth)
        gathered = jnp.take(flat, return_index, axis=0)
        corr = gathered.transpose(1, 0, 2, 3).reshape(thin, total_y, depth)
        corr = jnp.einsum("ji,xjz->xiz", m_y, corr, precision=HIGH)
        logs = lax.psum(jnp.log(corr), "view")
        est = est * jnp.exp(logs / views)
    return est


def solution(mesh):
    in_specs = (
        P("block", None, None),
        P("view", "block", None, None, None),
        P("view", None),
        P("view", None),
        P("view", None),
        P("view", None, None),
    )
    out_specs = P("block", None, None)
    return jax.shard_map(
        on_device, mesh=mesh, in_specs=in_specs, out_specs=out_specs, check_vma=False
    )
```

```python
import functools

import jax
import jax.numpy as jnp
from jax import lax
from jax.experimental import pallas as pl
from jax.experimental.pallas import tpu as pltpu
from jax.sharding import PartitionSpec as P

ITERS = 2

HIGH = lax.Precision.HIGHEST

SIDE = 8
LANES = 128
DATA_ROWS = 16
EST_ROWS = 4
META = DATA_ROWS + EST_ROWS
PACKET = META + 1
ORDER = (
    *((1, 5), (0, 2), (0, 1), (0, 6), (1, 1), (1, 2), (0, 4), (1, 4)),
    *((0, 5), (1, 0), (0, 7), (0, 0), (1, 3), (1, 6), (0, 3), (1, 7)),
)
LATE = {(g, b): int(b >= 4) for g, b in ORDER}


def lane_ids(rows):
    return lax.broadcasted_iota(jnp.int32, (rows, LANES), 1)


def row_ids(rows):
    return lax.broadcasted_iota(jnp.int32, (rows, LANES), 0)


def pack_kernel(copies, own, est, data, tx, ty, tz, out, meta):
    group = lax.axis_index("view") >> 1
    width = tx.shape[1]
    meta[...] = jnp.zeros_like(meta)
    meta[:, 3 * width : 3 * width + SIDE] = own[...].astype(jnp.float32)
    for k, taps in enumerate((tx, ty, tz)):
        meta[:, k * width : (k + 1) * width] = taps[...]
    row = meta[...]
    share = jnp.where(group == 0, est[:EST_ROWS, :], est[EST_ROWS:, :])
    lower, upper = data[:SIDE], data[SIDE:]
    for k in range(copies):
        at = k * PACKET
        out[at : at + SIDE, :] = lower
        out[at + SIDE : at + DATA_ROWS, :] = upper
        out[at + DATA_ROWS : at + META, :] = share
        out[at + META : at + PACKET, :] = row


def halves(value):
    high = value.astype(jnp.bfloat16)
    low = (value - high.astype(jnp.float32)).astype(jnp.bfloat16)
    return high, low


def matmul(a, b):
    return jnp.dot(a, b, preferred_element_type=jnp.float32)


def left(value):
    high, low = halves(value)
    return jnp.concatenate([high, low, high], axis=1)


def right(value):
    high, low = halves(value)
    return jnp.concatenate([high, high, low], axis=0)


def lane_pick(tile, index):
    return jnp.take_along_axis(tile, index, axis=1)


def placed(slabs, ref, groups, slots, flip):
    for p, (g, b) in enumerate(ORDER):
        v = (LATE[g, b] ^ flip) * groups + g
        for s in range(2):
            at = p * PACKET + s * SIDE
            slab = ref[at : at + SIDE, :]
            for y in range(SIDE):
                slabs[v][y] = jnp.where(slots[v][y] == 2 * b + s, slab, slabs[v][y])


def slot_numbers(owners):
    numbers = []
    for y, mine in enumerate(owners):
        place = jnp.zeros_like(mine)
        for other in owners[:y]:
            place += jnp.where(other == mine, 1.0, 0.0)
        numbers.append(2.0 * mine + place)
    return numbers


def spread_rows(tile):
    return [jnp.broadcast_to(tile[y : y + 1, :], (SIDE, LANES)) for y in range(SIDE)]


def blur(est, forward_depth, forward_side, views):
    deep = matmul(left(est), forward_depth)
    deep = [right(deep[:, v * LANES : (v + 1) * LANES]) for v in views]
    return [matmul(forward_side[v], deep[v]) for v in views]


def prepare_kernel(
    groups, reach, near, est_out, inverse, slabs_out, slots_out, forward_depth, forward_side, back_side, own_side, back_depth
):
    width = 2 * reach + 1
    block = lax.axis_index("block")
    views = range(2 * groups)
    for p, (g, b) in enumerate(ORDER):
        for i in range(EST_ROWS):
            y, at = g * EST_ROWS + i, p * PACKET + DATA_ROWS + i
            est_out[y * SIDE + b : y * SIDE + b + 1, :] = near[at : at + 1, :]
    est = est_out[...]

    lane, row = lane_ids(SIDE), row_ids(SIDE)
    lane_x, lane_y = lane & (SIDE - 1), lane >> 3
    signed = jnp.where(lane < LANES // 2, lane, lane - LANES)

    def kernel_row(meta, which, offset):
        inside = (offset >= -reach) & (offset <= reach)
        index = jnp.clip(offset, -reach, reach) + (which * width + reach)
        return jnp.where(inside, lane_pick(meta, index), 0.0)

    band = jnp.abs(lane_ids(LANES) - row_ids(LANES)) <= reach

    def toeplitz(base):
        rolled = pltpu.roll(jnp.tile(base, (LANES // SIDE, 1)), 0, 1, stride=1, stride_axis=0)
        return jnp.where(band, rolled, 0.0)

    metas = []
    for v in views:
        p = [(LATE[key], key[0]) for key in ORDER].index((v // groups, v % groups))
        at = p * PACKET + META
        metas.append(jnp.broadcast_to(near[at : at + 1, :], (SIDE, LANES)))
    depth = [kernel_row(meta, 2, -signed) for meta in metas]
    ahead = [
        (kernel_row(meta, 0, lane_x - row), kernel_row(meta, 1, lane_y - row)) for meta in metas
    ]
    owners = [lane_pick(meta, row + 3 * width) for meta in metas]
    depth_back = [kernel_row(meta, 2, signed) for meta in metas]
    back_y = [kernel_row(meta, 1, row - lane_y) for meta in metas]
    back_x = [kernel_row(meta, 0, row - lane_x) for meta in metas]
    own_x = [kernel_row(meta, 0, block - lane_x) for meta in metas]

    def side_matrix(x_tile, y_tile):
        side = jnp.concatenate([x_tile * y_row for y_row in spread_rows(y_tile)], axis=0)
        return left(side[:, : SIDE * SIDE])

    forward = jnp.concatenate([right(toeplitz(base)) for base in depth], axis=1)
    sides = [side_matrix(x_tile, y_tile) for x_tile, y_tile in ahead]
    blurred = blur(est, forward, sides, views)
    slots = [slot_numbers(spread_rows(tile)) for tile in owners]
    slabs = [[jnp.zeros((SIDE, LANES), jnp.float32)] * SIDE for _ in views]
    placed(slabs, near, groups, slots, 0)
    forward_depth[...] = forward
    for v in views:
        forward_side[v] = sides[v]
        back_side[v] = side_matrix(back_x[v], back_y[v])
        own = own_x[v] * back_y[v]
        own_side[v] = left(jnp.concatenate([own, own], axis=0)[:, : SIDE * SIDE])
        back_depth[:, v * LANES : (v + 1) * LANES] = right(toeplitz(depth_back[v]))
        slabs_out[v] = jnp.concatenate(slabs[v], axis=0)
        slots_out[v] = jnp.concatenate(slots[v], axis=0)
    for v in views:
        inverse[v] = 1.0 / blurred[v]


def finish_kernel(
    groups,
    far,
    est_in,
    inverse,
    slabs_in,
    slots_in,
    forward_depth,
    forward_side,
    back_side,
    own_side,
    back_depth,
    out,
    held,
):
    block = lax.axis_index("block")
    views = range(2 * groups)
    slabs = [[slabs_in[v, y * SIDE : (y + 1) * SIDE, :] for y in range(SIDE)] for v in views]
    slots = [[slots_in[v, y * SIDE : (y + 1) * SIDE, :] for y in range(SIDE)] for v in views]
    placed(slabs, far, groups, slots, 1)
    recorded = [jnp.concatenate(slabs[v], axis=0) for v in views]
    est = est_in[...]
    for step in range(ITERS):
        if step == 0:
            ratios = [recorded[v] * inverse[v] for v in views]
        else:
            blurred = blur(est, forward_depth[...], [forward_side[v] for v in views], views)
            ratios = [recorded[v] / blurred[v] for v in views]
        ratios = [right(ratios[v]) for v in views]
        last = step == ITERS - 1
        back = own_side if last else back_side
        spread = [left(matmul(back[v], ratios[v])) for v in views]
        corr = [matmul(spread[v], back_depth[:, v * LANES : (v + 1) * LANES]) for v in views]
        if last:
            corr = [value[:SIDE] for value in corr]
            held[: SIDE * SIDE, :] = est
            est = held[pl.ds(block, SIDE, stride=SIDE), :]
        roots = [lax.rsqrt(corr[v] * corr[v + 1]) for v in views[::2]]
        est = est * lax.rsqrt(roots[0] * roots[1])
    out[...] = est


def in_vmem(value):
    return pltpu.with_memory_space_constraint(value, pltpu.VMEM)


def on_device_small(estimate, view_data, taps_x, taps_y, taps_z, owner):
    blocks = lax.axis_size("block")
    views = lax.axis_size("view")
    width = taps_x.shape[1]
    groups = views // 2
    copies = groups * blocks
    vmem = pl.BlockSpec(memory_space=pltpu.VMEM)
    packet = pl.pallas_call(
        functools.partial(pack_kernel, copies),
        out_shape=pltpu.VMEM((copies * PACKET, LANES), jnp.float32),
        in_specs=[vmem] * 6,
        out_specs=vmem,
        scratch_shapes=[pltpu.VMEM((1, LANES), jnp.float32)],
        name="pack",
    )(owner.reshape(1, SIDE), estimate.reshape(SIDE, LANES), view_data.reshape(DATA_ROWS, LANES), taps_x, taps_y, taps_z)
    alike = [[(2 * g + (k ^ LATE[g, b])) * blocks + b for g, b in ORDER] for k in range(2)]
    near = lax.all_to_all(
        packet.reshape(copies, PACKET, 1, LANES), ("view", "block"), 0, 0, axis_index_groups=alike, tiled=True
    )
    near = near.reshape(copies * PACKET, LANES)
    far = lax.ppermute(near, "view", [(v, v ^ 1) for v in range(views)])
    wide = jnp.bfloat16
    prepared = pl.pallas_call(
        functools.partial(prepare_kernel, groups, width // 2),
        out_shape=[
            pltpu.VMEM((SIDE * SIDE, LANES), jnp.float32),
            pltpu.VMEM((views, SIDE * SIDE, LANES), jnp.float32),
            pltpu.VMEM((views, SIDE * SIDE, LANES), jnp.float32),
            pltpu.VMEM((views, SIDE * SIDE, LANES), jnp.float32),
            pltpu.VMEM((3 * LANES, views * LANES), wide),
            pltpu.VMEM((views, SIDE * SIDE, 3 * SIDE * SIDE), wide),
            pltpu.VMEM((views, SIDE * SIDE, 3 * SIDE * SIDE), wide),
            pltpu.VMEM((views, 2 * SIDE, 3 * SIDE * SIDE), wide),
            pltpu.VMEM((3 * LANES, views * LANES), wide),
        ],
        in_specs=[vmem],
        out_specs=[vmem] * 9,
        name="prepare",
    )(in_vmem(near))
    joined = pl.pallas_call(
        functools.partial(finish_kernel, groups),
        out_shape=jax.ShapeDtypeStruct((SIDE, LANES), jnp.float32),
        in_specs=[vmem] * 10,
        out_specs=vmem,
        scratch_shapes=[pltpu.VMEM((2 * SIDE * SIDE, LANES), jnp.float32)],
        name="finish",
    )(in_vmem(far), *[in_vmem(value) for value in prepared])
    return joined.reshape(estimate.shape)


def fits_one_device(estimate, view_data, taps_x, blocks, views):
    thin, total_y, depth = estimate.shape
    return (
        (thin, blocks, total_y, depth) == (1, SIDE, SIDE, LANES)
        and view_data.shape[1] == 2
        and views == 4
        and taps_x.shape[1] % 2 == 1
        and 3 * taps_x.shape[1] + SIDE <= LANES
    )


def band_matrix(taps, length):
    width = taps.shape[0]
    reach = width // 2
    rows = jnp.arange(length, dtype=jnp.int32)[:, None]
    cols = jnp.arange(length, dtype=jnp.int32)[None, :]
    offset = cols - rows + reach
    inside = (offset >= 0) & (offset < width)
    index = jnp.clip(offset, 0, width - 1)
    values = jnp.take(taps, index.reshape(-1), axis=0).reshape(length, length)
    return jnp.where(inside, values, jnp.zeros_like(values))


def on_device(estimate, view_data, taps_x, taps_y, taps_z, owner):
    blocks = lax.axis_size("block")
    views = lax.axis_size("view")
    if fits_one_device(estimate, view_data, taps_x, blocks, views):
        return on_device_small(estimate, view_data, taps_x, taps_y, taps_z, owner)
    thin = estimate.shape[0]
    total_y = estimate.shape[1]
    depth = estimate.shape[2]
    total_x = thin * blocks
    slots = view_data.shape[1]
    own = owner[0, :, 0]
    order = jnp.arange(blocks, dtype=jnp.int32)
    earlier = (own[:, None] == own[None, :]) & (order[None, :] < order[:, None])
    place = jnp.sum(earlier.astype(jnp.int32), axis=1)
    slot_ids = jnp.arange(slots, dtype=jnp.int32)
    hits = (place[None, None, :] == slot_ids[:, None, None]) & (
        own[None, None, :] == order[None, :, None]
    )
    filled = jnp.any(hits, axis=2).astype(jnp.float32)
    source_slab = jnp.sum(jnp.where(hits, order[None, None, :], 0), axis=2)
    return_index = place * blocks + own
    device = lax.axis_index("block")
    held = jnp.sum((own == device).astype(jnp.int32))
    live = (slot_ids < held)[:, None, None, None]
    m_x = band_matrix(taps_x[0], total_x)
    m_y = band_matrix(taps_y[0], total_y)
    m_z = band_matrix(taps_z[0], depth)
    recorded = view_data[0]
    est = estimate
    for step in range(ITERS):
        forward = jnp.einsum("ij,xjz->xiz", m_y, est, precision=HIGH)
        pieces = forward.reshape(thin, blocks, thin, depth)
        picked = jnp.take(pieces, source_slab.reshape(-1), axis=1)
        picked = picked.reshape(thin, slots, blocks, thin, depth).transpose(1, 2, 0, 3, 4)
        picked = picked * filled[:, :, None, None, None]
        arrived = lax.all_to_all(picked, "block", split_axis=1, concat_axis=1, tiled=True)
        held_est = arrived.reshape(slots, total_x, thin, depth)
        blurred = jnp.einsum("ij,sjyz->siyz", m_x, held_est, precision=HIGH)
        blurred = jnp.einsum("sxyj,ij->sxyi", blurred, m_z, precision=HIGH)
        ratio = jnp.where(live, recorded / jnp.where(live, blurred, 1.0), 0.0)
        back = jnp.einsum("ji,sjyz->siyz", m_x, ratio, precision=HIGH)
        back = jnp.einsum("sxyj,ji->sxyi", back, m_z, precision=HIGH)
        returned = lax.all_to_all(
            back.reshape(slots, blocks, thin, thin, depth),
            "block",
            split_axis=1,
            concat_axis=1,
            tiled=True,
        )
        flat = returned.reshape(slots * blocks, thin, thin, depth)
        gathered = jnp.take(flat, return_index, axis=0)
        corr = gathered.transpose(1, 0, 2, 3).reshape(thin, total_y, depth)
        corr = jnp.einsum("ji,xjz->xiz", m_y, corr, precision=HIGH)
        logs = lax.psum(jnp.log(corr), "view")
        est = est * jnp.exp(logs / views)
    return est


def solution(mesh):
    in_specs = (
        P("block", None, None),
        P("view", "block", None, None, None),
        P("view", None),
        P("view", None),
        P("view", None),
        P("view", None, None),
    )
    out_specs = P("block", None, None)
    return jax.shard_map(
        on_device, mesh=mesh, in_specs=in_specs, out_specs=out_specs, check_vma=False
    )
```

```python
import functools

import jax
import jax.numpy as jnp
from jax import lax
from jax.experimental import pallas as pl
from jax.experimental.pallas import tpu as pltpu
from jax.sharding import PartitionSpec as P

ITERS = 2

HIGH = lax.Precision.HIGHEST

SIDE = 8
LANES = 128
DATA_ROWS = 16
EST_ROWS = 4
META = DATA_ROWS + EST_ROWS
PACKET = META + 1
ORDER = (
    *((1, 5), (0, 2), (0, 1), (0, 6), (1, 1), (1, 2), (0, 4), (1, 4)),
    *((0, 5), (1, 0), (0, 7), (0, 0), (1, 3), (1, 6), (0, 3), (1, 7)),
)
LATE = {(g, b): int(b >= 4) for g, b in ORDER}


def lane_ids(rows):
    return lax.broadcasted_iota(jnp.int32, (rows, LANES), 1)


def row_ids(rows):
    return lax.broadcasted_iota(jnp.int32, (rows, LANES), 0)


def pack_kernel(copies, own, est, data, tx, ty, tz, out, meta):
    group = lax.axis_index("view") >> 1
    width = tx.shape[1]
    meta[...] = jnp.zeros_like(meta)
    meta[:, 3 * width : 3 * width + SIDE] = own[...].astype(jnp.float32)
    for k, taps in enumerate((tx, ty, tz)):
        meta[:, k * width : (k + 1) * width] = taps[...]
    row = meta[...]
    share = jnp.where(group == 0, est[:EST_ROWS, :], est[EST_ROWS:, :])
    lower, upper = data[:SIDE], data[SIDE:]
    for k in range(copies):
        at = k * PACKET
        out[at : at + SIDE, :] = lower
        out[at + SIDE : at + DATA_ROWS, :] = upper
        out[at + DATA_ROWS : at + META, :] = share
        out[at + META : at + PACKET, :] = row


def halves(value):
    high = value.astype(jnp.bfloat16)
    low = (value - high.astype(jnp.float32)).astype(jnp.bfloat16)
    return high, low


def matmul(a, b):
    return jnp.dot(a, b, preferred_element_type=jnp.float32)


def left(value):
    high, low = halves(value)
    return jnp.concatenate([high, low, high], axis=1)


def right(value):
    high, low = halves(value)
    return jnp.concatenate([high, high, low], axis=0)


def lane_pick(tile, index):
    return jnp.take_along_axis(tile, index, axis=1)


def placed(slabs, ref, length, groups, slots, flip):
    for p, (g, b) in enumerate(ORDER):
        v = (LATE[g, b] ^ flip) * groups + g
        for s in range(2):
            at = p * length + s * SIDE
            slab = ref[at : at + SIDE, :]
            for y in range(SIDE):
                slabs[v][y] = jnp.where(slots[v][y] == 2 * b + s, slab, slabs[v][y])


def slot_numbers(owners):
    numbers = []
    for y, mine in enumerate(owners):
        place = jnp.zeros_like(mine)
        for other in owners[:y]:
            place += jnp.where(other == mine, 1.0, 0.0)
        numbers.append(2.0 * mine + place)
    return numbers


def spread_rows(tile):
    return [jnp.broadcast_to(tile[y : y + 1, :], (SIDE, LANES)) for y in range(SIDE)]


def blur(est, forward_depth, forward_side, views):
    deep = matmul(left(est), forward_depth)
    deep = [right(deep[:, v * LANES : (v + 1) * LANES]) for v in views]
    return [matmul(forward_side[v], deep[v]) for v in views]


def prepare_kernel(
    groups, reach, near, est_out, inverse, slabs_out, slots_out, forward_depth, forward_side, back_side, own_side, back_depth
):
    width = 2 * reach + 1
    block = lax.axis_index("block")
    views = range(2 * groups)
    for p, (g, b) in enumerate(ORDER):
        for i in range(EST_ROWS):
            y, at = g * EST_ROWS + i, p * PACKET + DATA_ROWS + i
            est_out[y * SIDE + b : y * SIDE + b + 1, :] = near[at : at + 1, :]
    est = est_out[...]

    lane, row = lane_ids(SIDE), row_ids(SIDE)
    lane_x, lane_y = lane & (SIDE - 1), lane >> 3
    signed = jnp.where(lane < LANES // 2, lane, lane - LANES)

    def kernel_row(meta, which, offset):
        inside = (offset >= -reach) & (offset <= reach)
        index = jnp.clip(offset, -reach, reach) + (which * width + reach)
        return jnp.where(inside, lane_pick(meta, index), 0.0)

    band = jnp.abs(lane_ids(LANES) - row_ids(LANES)) <= reach

    def toeplitz(base):
        rolled = pltpu.roll(jnp.tile(base, (LANES // SIDE, 1)), 0, 1, stride=1, stride_axis=0)
        return jnp.where(band, rolled, 0.0)

    metas = []
    for v in views:
        p = [(LATE[key], key[0]) for key in ORDER].index((v // groups, v % groups))
        at = p * PACKET + META
        metas.append(jnp.broadcast_to(near[at : at + 1, :], (SIDE, LANES)))
    depth = [kernel_row(meta, 2, -signed) for meta in metas]
    ahead = [
        (kernel_row(meta, 0, lane_x - row), kernel_row(meta, 1, lane_y - row)) for meta in metas
    ]
    owners = [lane_pick(meta, row + 3 * width) for meta in metas]
    depth_back = [kernel_row(meta, 2, signed) for meta in metas]
    back_y = [kernel_row(meta, 1, row - lane_y) for meta in metas]
    back_x = [kernel_row(meta, 0, row - lane_x) for meta in metas]
    own_x = [kernel_row(meta, 0, block - lane_x) for meta in metas]

    def side_matrix(x_tile, y_tile):
        side = jnp.concatenate([x_tile * y_row for y_row in spread_rows(y_tile)], axis=0)
        return left(side[:, : SIDE * SIDE])

    forward = jnp.concatenate([right(toeplitz(base)) for base in depth], axis=1)
    sides = [side_matrix(x_tile, y_tile) for x_tile, y_tile in ahead]
    blurred = blur(est, forward, sides, views)
    slots = [slot_numbers(spread_rows(tile)) for tile in owners]
    slabs = [[jnp.zeros((SIDE, LANES), jnp.float32)] * SIDE for _ in views]
    placed(slabs, near, PACKET, groups, slots, 0)
    forward_depth[...] = forward
    for v in views:
        forward_side[v] = sides[v]
        back_side[v] = side_matrix(back_x[v], back_y[v])
        own = own_x[v] * back_y[v]
        own_side[v] = left(jnp.concatenate([own, own], axis=0)[:, : SIDE * SIDE])
        back_depth[:, v * LANES : (v + 1) * LANES] = right(toeplitz(depth_back[v]))
        slabs_out[v] = jnp.concatenate(slabs[v], axis=0)
        slots_out[v] = jnp.concatenate(slots[v], axis=0)
    for v in views:
        inverse[v] = 1.0 / blurred[v]


def finish_kernel(
    groups,
    far,
    est_in,
    inverse,
    slabs_in,
    slots_in,
    forward_depth,
    forward_side,
    back_side,
    own_side,
    back_depth,
    out,
    held,
):
    block = lax.axis_index("block")
    views = range(2 * groups)
    slabs = [[slabs_in[v, y * SIDE : (y + 1) * SIDE, :] for y in range(SIDE)] for v in views]
    slots = [[slots_in[v, y * SIDE : (y + 1) * SIDE, :] for y in range(SIDE)] for v in views]
    placed(slabs, far, DATA_ROWS, groups, slots, 1)
    recorded = [jnp.concatenate(slabs[v], axis=0) for v in views]
    est = est_in[...]
    for step in range(ITERS):
        if step == 0:
            ratios = [recorded[v] * inverse[v] for v in views]
        else:
            blurred = blur(est, forward_depth[...], [forward_side[v] for v in views], views)
            ratios = [recorded[v] / blurred[v] for v in views]
        ratios = [right(ratios[v]) for v in views]
        last = step == ITERS - 1
        back = own_side if last else back_side
        spread = [left(matmul(back[v], ratios[v])) for v in views]
        corr = [matmul(spread[v], back_depth[:, v * LANES : (v + 1) * LANES]) for v in views]
        if last:
            corr = [value[:SIDE] for value in corr]
            held[: SIDE * SIDE, :] = est
            est = held[pl.ds(block, SIDE, stride=SIDE), :]
        roots = [lax.rsqrt(corr[v] * corr[v + 1]) for v in views[::2]]
        est = est * lax.rsqrt(roots[0] * roots[1])
    out[...] = est


def in_vmem(value):
    return pltpu.with_memory_space_constraint(value, pltpu.VMEM)


def on_device_small(estimate, view_data, taps_x, taps_y, taps_z, owner):
    blocks = lax.axis_size("block")
    views = lax.axis_size("view")
    width = taps_x.shape[1]
    groups = views // 2
    copies = groups * blocks
    vmem = pl.BlockSpec(memory_space=pltpu.VMEM)
    packet = pl.pallas_call(
        functools.partial(pack_kernel, copies),
        out_shape=pltpu.VMEM((copies * PACKET, LANES), jnp.float32),
        in_specs=[vmem] * 6,
        out_specs=vmem,
        scratch_shapes=[pltpu.VMEM((1, LANES), jnp.float32)],
        name="pack",
    )(owner.reshape(1, SIDE), estimate.reshape(SIDE, LANES), view_data.reshape(DATA_ROWS, LANES), taps_x, taps_y, taps_z)
    alike = [[(2 * g + (k ^ LATE[g, b])) * blocks + b for g, b in ORDER] for k in range(2)]
    near = lax.all_to_all(
        packet.reshape(copies, PACKET, 1, LANES), ("view", "block"), 0, 0, axis_index_groups=alike, tiled=True
    )
    far = near[:, :DATA_ROWS].reshape(copies * DATA_ROWS, LANES)
    far = lax.ppermute(far, "view", [(v, v ^ 1) for v in range(views)])
    near = near.reshape(copies * PACKET, LANES)
    wide = jnp.bfloat16
    prepared = pl.pallas_call(
        functools.partial(prepare_kernel, groups, width // 2),
        out_shape=[
            pltpu.VMEM((SIDE * SIDE, LANES), jnp.float32),
            pltpu.VMEM((views, SIDE * SIDE, LANES), jnp.float32),
            pltpu.VMEM((views, SIDE * SIDE, LANES), jnp.float32),
            pltpu.VMEM((views, SIDE * SIDE, LANES), jnp.float32),
            pltpu.VMEM((3 * LANES, views * LANES), wide),
            pltpu.VMEM((views, SIDE * SIDE, 3 * SIDE * SIDE), wide),
            pltpu.VMEM((views, SIDE * SIDE, 3 * SIDE * SIDE), wide),
            pltpu.VMEM((views, 2 * SIDE, 3 * SIDE * SIDE), wide),
            pltpu.VMEM((3 * LANES, views * LANES), wide),
        ],
        in_specs=[vmem],
        out_specs=[vmem] * 9,
        name="prepare",
    )(in_vmem(near))
    joined = pl.pallas_call(
        functools.partial(finish_kernel, groups),
        out_shape=jax.ShapeDtypeStruct((SIDE, LANES), jnp.float32),
        in_specs=[vmem] * 10,
        out_specs=vmem,
        scratch_shapes=[pltpu.VMEM((2 * SIDE * SIDE, LANES), jnp.float32)],
        name="finish",
    )(in_vmem(far), *[in_vmem(value) for value in prepared])
    return joined.reshape(estimate.shape)


def fits_one_device(estimate, view_data, taps_x, blocks, views):
    thin, total_y, depth = estimate.shape
    return (
        (thin, blocks, total_y, depth) == (1, SIDE, SIDE, LANES)
        and view_data.shape[1] == 2
        and views == 4
        and taps_x.shape[1] % 2 == 1
        and 3 * taps_x.shape[1] + SIDE <= LANES
    )


def band_matrix(taps, length):
    width = taps.shape[0]
    reach = width // 2
    rows = jnp.arange(length, dtype=jnp.int32)[:, None]
    cols = jnp.arange(length, dtype=jnp.int32)[None, :]
    offset = cols - rows + reach
    inside = (offset >= 0) & (offset < width)
    index = jnp.clip(offset, 0, width - 1)
    values = jnp.take(taps, index.reshape(-1), axis=0).reshape(length, length)
    return jnp.where(inside, values, jnp.zeros_like(values))


def on_device(estimate, view_data, taps_x, taps_y, taps_z, owner):
    blocks = lax.axis_size("block")
    views = lax.axis_size("view")
    if fits_one_device(estimate, view_data, taps_x, blocks, views):
        return on_device_small(estimate, view_data, taps_x, taps_y, taps_z, owner)
    thin = estimate.shape[0]
    total_y = estimate.shape[1]
    depth = estimate.shape[2]
    total_x = thin * blocks
    slots = view_data.shape[1]
    own = owner[0, :, 0]
    order = jnp.arange(blocks, dtype=jnp.int32)
    earlier = (own[:, None] == own[None, :]) & (order[None, :] < order[:, None])
    place = jnp.sum(earlier.astype(jnp.int32), axis=1)
    slot_ids = jnp.arange(slots, dtype=jnp.int32)
    hits = (place[None, None, :] == slot_ids[:, None, None]) & (
        own[None, None, :] == order[None, :, None]
    )
    filled = jnp.any(hits, axis=2).astype(jnp.float32)
    source_slab = jnp.sum(jnp.where(hits, order[None, None, :], 0), axis=2)
    return_index = place * blocks + own
    device = lax.axis_index("block")
    held = jnp.sum((own == device).astype(jnp.int32))
    live = (slot_ids < held)[:, None, None, None]
    m_x = band_matrix(taps_x[0], total_x)
    m_y = band_matrix(taps_y[0], total_y)
    m_z = band_matrix(taps_z[0], depth)
    recorded = view_data[0]
    est = estimate
    for step in range(ITERS):
        forward = jnp.einsum("ij,xjz->xiz", m_y, est, precision=HIGH)
        pieces = forward.reshape(thin, blocks, thin, depth)
        picked = jnp.take(pieces, source_slab.reshape(-1), axis=1)
        picked = picked.reshape(thin, slots, blocks, thin, depth).transpose(1, 2, 0, 3, 4)
        picked = picked * filled[:, :, None, None, None]
        arrived = lax.all_to_all(picked, "block", split_axis=1, concat_axis=1, tiled=True)
        held_est = arrived.reshape(slots, total_x, thin, depth)
        blurred = jnp.einsum("ij,sjyz->siyz", m_x, held_est, precision=HIGH)
        blurred = jnp.einsum("sxyj,ij->sxyi", blurred, m_z, precision=HIGH)
        ratio = jnp.where(live, recorded / jnp.where(live, blurred, 1.0), 0.0)
        back = jnp.einsum("ji,sjyz->siyz", m_x, ratio, precision=HIGH)
        back = jnp.einsum("sxyj,ji->sxyi", back, m_z, precision=HIGH)
        returned = lax.all_to_all(
            back.reshape(slots, blocks, thin, thin, depth),
            "block",
            split_axis=1,
            concat_axis=1,
            tiled=True,
        )
        flat = returned.reshape(slots * blocks, thin, thin, depth)
        gathered = jnp.take(flat, return_index, axis=0)
        corr = gathered.transpose(1, 0, 2, 3).reshape(thin, total_y, depth)
        corr = jnp.einsum("ji,xjz->xiz", m_y, corr, precision=HIGH)
        logs = lax.psum(jnp.log(corr), "view")
        est = est * jnp.exp(logs / views)
    return est


def solution(mesh):
    in_specs = (
        P("block", None, None),
        P("view", "block", None, None, None),
        P("view", None),
        P("view", None),
        P("view", None),
        P("view", None, None),
    )
    out_specs = P("block", None, None)
    return jax.shard_map(
        on_device, mesh=mesh, in_specs=in_specs, out_specs=out_specs, check_vma=False
    )
```

```python
import functools

import jax
import jax.numpy as jnp
from jax import lax
from jax.experimental import pallas as pl
from jax.experimental.pallas import tpu as pltpu
from jax.sharding import PartitionSpec as P

ITERS = 2

HIGH = lax.Precision.HIGHEST

SIDE = 8
LANES = 128
DATA_ROWS = 16
EST_ROWS = 4
META = DATA_ROWS + EST_ROWS
PACKET = META + 1
ORDER = (
    *((1, 5), (0, 2), (0, 1), (0, 6), (1, 1), (1, 2), (0, 4), (1, 4)),
    *((0, 5), (1, 0), (0, 7), (0, 0), (1, 3), (1, 6), (0, 3), (1, 7)),
)
LATE = {(g, b): int(b >= 4) for g, b in ORDER}


def lane_ids(rows):
    return lax.broadcasted_iota(jnp.int32, (rows, LANES), 1)


def row_ids(rows):
    return lax.broadcasted_iota(jnp.int32, (rows, LANES), 0)


def pack_kernel(copies, own, est, data, tx, ty, tz, out, meta):
    group = lax.axis_index("view") >> 1
    width = tx.shape[1]
    meta[...] = jnp.zeros_like(meta)
    meta[:, 3 * width : 3 * width + SIDE] = own[...].astype(jnp.float32)
    for k, taps in enumerate((tx, ty, tz)):
        meta[:, k * width : (k + 1) * width] = taps[...]
    row = meta[...]
    share = jnp.where(group == 0, est[:EST_ROWS, :], est[EST_ROWS:, :])
    lower, upper = data[:SIDE], data[SIDE:]
    for k in range(copies):
        at = k * PACKET
        out[at : at + SIDE, :] = lower
        out[at + SIDE : at + DATA_ROWS, :] = upper
        out[at + DATA_ROWS : at + META, :] = share
        out[at + META : at + PACKET, :] = row


def halves(value):
    high = value.astype(jnp.bfloat16)
    low = (value - high.astype(jnp.float32)).astype(jnp.bfloat16)
    return high, low


def matmul(a, b):
    return jnp.dot(a, b, preferred_element_type=jnp.float32)


def left(value):
    high, low = halves(value)
    return jnp.concatenate([high, high, low], axis=1)


def right(value):
    high, low = halves(value)
    return jnp.concatenate([high, low, high], axis=0)


def lane_pick(tile, index):
    return jnp.take_along_axis(tile, index, axis=1)


def placed(slabs, ref, length, groups, slots, flip):
    for p, (g, b) in enumerate(ORDER):
        v = (LATE[g, b] ^ flip) * groups + g
        for s in range(2):
            at = p * length + s * SIDE
            slab = ref[at : at + SIDE, :]
            for y in range(SIDE):
                slabs[v][y] = jnp.where(slots[v][y] == 2 * b + s, slab, slabs[v][y])


def slot_numbers(owners):
    numbers = []
    for y, mine in enumerate(owners):
        place = jnp.zeros_like(mine)
        for other in owners[:y]:
            place += jnp.where(other == mine, 1.0, 0.0)
        numbers.append(2.0 * mine + place)
    return numbers


def spread_rows(tile):
    return [jnp.broadcast_to(tile[y : y + 1, :], (SIDE, LANES)) for y in range(SIDE)]


def blur(est, forward_depth, forward_side, views):
    deep = matmul(left(est), forward_depth)
    deep = [right(deep[:, v * LANES : (v + 1) * LANES]) for v in views]
    return [matmul(forward_side[v], deep[v]) for v in views]


def prepare_kernel(
    groups, reach, near, est_out, inverse, slabs_out, slots_out, forward_depth, forward_side, back_side, own_side, back_depth
):
    width = 2 * reach + 1
    block = lax.axis_index("block")
    views = range(2 * groups)
    for p, (g, b) in enumerate(ORDER):
        for i in range(EST_ROWS):
            y, at = g * EST_ROWS + i, p * PACKET + DATA_ROWS + i
            est_out[y * SIDE + b : y * SIDE + b + 1, :] = near[at : at + 1, :]
    est = est_out[...]

    lane, row = lane_ids(SIDE), row_ids(SIDE)
    lane_x, lane_y = lane & (SIDE - 1), lane >> 3
    signed = jnp.where(lane < LANES // 2, lane, lane - LANES)

    def kernel_row(meta, which, offset):
        inside = (offset >= -reach) & (offset <= reach)
        index = jnp.clip(offset, -reach, reach) + (which * width + reach)
        return jnp.where(inside, lane_pick(meta, index), 0.0)

    band = jnp.abs(lane_ids(LANES) - row_ids(LANES)) <= reach

    def toeplitz(base):
        rolled = pltpu.roll(jnp.tile(base, (LANES // SIDE, 1)), 0, 1, stride=1, stride_axis=0)
        return jnp.where(band, rolled, 0.0)

    metas = []
    for v in views:
        p = [(LATE[key], key[0]) for key in ORDER].index((v // groups, v % groups))
        at = p * PACKET + META
        metas.append(jnp.broadcast_to(near[at : at + 1, :], (SIDE, LANES)))
    depth = [kernel_row(meta, 2, -signed) for meta in metas]
    ahead = [
        (kernel_row(meta, 0, lane_x - row), kernel_row(meta, 1, lane_y - row)) for meta in metas
    ]
    owners = [lane_pick(meta, row + 3 * width) for meta in metas]
    depth_back = [kernel_row(meta, 2, signed) for meta in metas]
    back_y = [kernel_row(meta, 1, row - lane_y) for meta in metas]
    back_x = [kernel_row(meta, 0, row - lane_x) for meta in metas]
    own_x = [kernel_row(meta, 0, block - lane_x) for meta in metas]

    def side_matrix(x_tile, y_tile):
        side = jnp.concatenate([x_tile * y_row for y_row in spread_rows(y_tile)], axis=0)
        return left(side[:, : SIDE * SIDE])

    forward = jnp.concatenate([right(toeplitz(base)) for base in depth], axis=1)
    sides = [side_matrix(x_tile, y_tile) for x_tile, y_tile in ahead]
    blurred = blur(est, forward, sides, views)
    slots = [slot_numbers(spread_rows(tile)) for tile in owners]
    slabs = [[jnp.zeros((SIDE, LANES), jnp.float32)] * SIDE for _ in views]
    placed(slabs, near, PACKET, groups, slots, 0)
    forward_depth[...] = forward
    for v in views:
        forward_side[v] = sides[v]
        back_side[v] = side_matrix(back_x[v], back_y[v])
        own = own_x[v] * back_y[v]
        own_side[v] = left(jnp.concatenate([own, own], axis=0)[:, : SIDE * SIDE])
        back_depth[:, v * LANES : (v + 1) * LANES] = right(toeplitz(depth_back[v]))
        slabs_out[v] = jnp.concatenate(slabs[v], axis=0)
        slots_out[v] = jnp.concatenate(slots[v], axis=0)
    for v in views:
        inverse[v] = 1.0 / blurred[v]


def finish_kernel(
    groups,
    far,
    est_in,
    inverse,
    slabs_in,
    slots_in,
    forward_depth,
    forward_side,
    back_side,
    own_side,
    back_depth,
    out,
    held,
):
    block = lax.axis_index("block")
    views = range(2 * groups)
    slabs = [[slabs_in[v, y * SIDE : (y + 1) * SIDE, :] for y in range(SIDE)] for v in views]
    slots = [[slots_in[v, y * SIDE : (y + 1) * SIDE, :] for y in range(SIDE)] for v in views]
    placed(slabs, far, DATA_ROWS, groups, slots, 1)
    recorded = [jnp.concatenate(slabs[v], axis=0) for v in views]
    est = est_in[...]
    for step in range(ITERS):
        if step == 0:
            ratios = [recorded[v] * inverse[v] for v in views]
        else:
            blurred = blur(est, forward_depth[...], [forward_side[v] for v in views], views)
            ratios = [recorded[v] / blurred[v] for v in views]
        ratios = [right(ratios[v]) for v in views]
        last = step == ITERS - 1
        back = own_side if last else back_side
        spread = [left(matmul(back[v], ratios[v])) for v in views]
        corr = [matmul(spread[v], back_depth[:, v * LANES : (v + 1) * LANES]) for v in views]
        if last:
            corr = [value[:SIDE] for value in corr]
            held[: SIDE * SIDE, :] = est
            est = held[pl.ds(block, SIDE, stride=SIDE), :]
        roots = [lax.rsqrt(corr[v] * corr[v + 1]) for v in views[::2]]
        est = est * lax.rsqrt(roots[0] * roots[1])
    out[...] = est


def in_vmem(value):
    return pltpu.with_memory_space_constraint(value, pltpu.VMEM)


def on_device_small(estimate, view_data, taps_x, taps_y, taps_z, owner):
    blocks = lax.axis_size("block")
    views = lax.axis_size("view")
    width = taps_x.shape[1]
    groups = views // 2
    copies = groups * blocks
    vmem = pl.BlockSpec(memory_space=pltpu.VMEM)
    packet = pl.pallas_call(
        functools.partial(pack_kernel, copies),
        out_shape=pltpu.VMEM((copies * PACKET, LANES), jnp.float32),
        in_specs=[vmem] * 6,
        out_specs=vmem,
        scratch_shapes=[pltpu.VMEM((1, LANES), jnp.float32)],
        name="pack",
    )(owner.reshape(1, SIDE), estimate.reshape(SIDE, LANES), view_data.reshape(DATA_ROWS, LANES), taps_x, taps_y, taps_z)
    alike = [[(2 * g + (k ^ LATE[g, b])) * blocks + b for g, b in ORDER] for k in range(2)]
    near = lax.all_to_all(
        packet.reshape(copies, PACKET, 1, LANES), ("view", "block"), 0, 0, axis_index_groups=alike, tiled=True
    )
    far = near[:, :DATA_ROWS].reshape(copies * DATA_ROWS, LANES)
    far = lax.ppermute(far, "view", [(v, v ^ 1) for v in range(views)])
    near = near.reshape(copies * PACKET, LANES)
    wide = jnp.bfloat16
    prepared = pl.pallas_call(
        functools.partial(prepare_kernel, groups, width // 2),
        out_shape=[
            pltpu.VMEM((SIDE * SIDE, LANES), jnp.float32),
            pltpu.VMEM((views, SIDE * SIDE, LANES), jnp.float32),
            pltpu.VMEM((views, SIDE * SIDE, LANES), jnp.float32),
            pltpu.VMEM((views, SIDE * SIDE, LANES), jnp.float32),
            pltpu.VMEM((3 * LANES, views * LANES), wide),
            pltpu.VMEM((views, SIDE * SIDE, 3 * SIDE * SIDE), wide),
            pltpu.VMEM((views, SIDE * SIDE, 3 * SIDE * SIDE), wide),
            pltpu.VMEM((views, 2 * SIDE, 3 * SIDE * SIDE), wide),
            pltpu.VMEM((3 * LANES, views * LANES), wide),
        ],
        in_specs=[vmem],
        out_specs=[vmem] * 9,
        name="prepare",
    )(in_vmem(near))
    joined = pl.pallas_call(
        functools.partial(finish_kernel, groups),
        out_shape=jax.ShapeDtypeStruct((SIDE, LANES), jnp.float32),
        in_specs=[vmem] * 10,
        out_specs=vmem,
        scratch_shapes=[pltpu.VMEM((2 * SIDE * SIDE, LANES), jnp.float32)],
        name="finish",
    )(in_vmem(far), *[in_vmem(value) for value in prepared])
    return joined.reshape(estimate.shape)


def fits_one_device(estimate, view_data, taps_x, blocks, views):
    thin, total_y, depth = estimate.shape
    return (
        (thin, blocks, total_y, depth) == (1, SIDE, SIDE, LANES)
        and view_data.shape[1] == 2
        and views == 4
        and taps_x.shape[1] % 2 == 1
        and 3 * taps_x.shape[1] + SIDE <= LANES
    )


def band_matrix(taps, length):
    width = taps.shape[0]
    reach = width // 2
    rows = jnp.arange(length, dtype=jnp.int32)[:, None]
    cols = jnp.arange(length, dtype=jnp.int32)[None, :]
    offset = cols - rows + reach
    inside = (offset >= 0) & (offset < width)
    index = jnp.clip(offset, 0, width - 1)
    values = jnp.take(taps, index.reshape(-1), axis=0).reshape(length, length)
    return jnp.where(inside, values, jnp.zeros_like(values))


def on_device(estimate, view_data, taps_x, taps_y, taps_z, owner):
    blocks = lax.axis_size("block")
    views = lax.axis_size("view")
    if fits_one_device(estimate, view_data, taps_x, blocks, views):
        return on_device_small(estimate, view_data, taps_x, taps_y, taps_z, owner)
    thin = estimate.shape[0]
    total_y = estimate.shape[1]
    depth = estimate.shape[2]
    total_x = thin * blocks
    slots = view_data.shape[1]
    own = owner[0, :, 0]
    order = jnp.arange(blocks, dtype=jnp.int32)
    earlier = (own[:, None] == own[None, :]) & (order[None, :] < order[:, None])
    place = jnp.sum(earlier.astype(jnp.int32), axis=1)
    slot_ids = jnp.arange(slots, dtype=jnp.int32)
    hits = (place[None, None, :] == slot_ids[:, None, None]) & (
        own[None, None, :] == order[None, :, None]
    )
    filled = jnp.any(hits, axis=2).astype(jnp.float32)
    source_slab = jnp.sum(jnp.where(hits, order[None, None, :], 0), axis=2)
    return_index = place * blocks + own
    device = lax.axis_index("block")
    held = jnp.sum((own == device).astype(jnp.int32))
    live = (slot_ids < held)[:, None, None, None]
    m_x = band_matrix(taps_x[0], total_x)
    m_y = band_matrix(taps_y[0], total_y)
    m_z = band_matrix(taps_z[0], depth)
    recorded = view_data[0]
    est = estimate
    for step in range(ITERS):
        forward = jnp.einsum("ij,xjz->xiz", m_y, est, precision=HIGH)
        pieces = forward.reshape(thin, blocks, thin, depth)
        picked = jnp.take(pieces, source_slab.reshape(-1), axis=1)
        picked = picked.reshape(thin, slots, blocks, thin, depth).transpose(1, 2, 0, 3, 4)
        picked = picked * filled[:, :, None, None, None]
        arrived = lax.all_to_all(picked, "block", split_axis=1, concat_axis=1, tiled=True)
        held_est = arrived.reshape(slots, total_x, thin, depth)
        blurred = jnp.einsum("ij,sjyz->siyz", m_x, held_est, precision=HIGH)
        blurred = jnp.einsum("sxyj,ij->sxyi", blurred, m_z, precision=HIGH)
        ratio = jnp.where(live, recorded / jnp.where(live, blurred, 1.0), 0.0)
        back = jnp.einsum("ji,sjyz->siyz", m_x, ratio, precision=HIGH)
        back = jnp.einsum("sxyj,ji->sxyi", back, m_z, precision=HIGH)
        returned = lax.all_to_all(
            back.reshape(slots, blocks, thin, thin, depth),
            "block",
            split_axis=1,
            concat_axis=1,
            tiled=True,
        )
        flat = returned.reshape(slots * blocks, thin, thin, depth)
        gathered = jnp.take(flat, return_index, axis=0)
        corr = gathered.transpose(1, 0, 2, 3).reshape(thin, total_y, depth)
        corr = jnp.einsum("ji,xjz->xiz", m_y, corr, precision=HIGH)
        logs = lax.psum(jnp.log(corr), "view")
        est = est * jnp.exp(logs / views)
    return est


def solution(mesh):
    in_specs = (
        P("block", None, None),
        P("view", "block", None, None, None),
        P("view", None),
        P("view", None),
        P("view", None),
        P("view", None, None),
    )
    out_specs = P("block", None, None)
    return jax.shard_map(
        on_device, mesh=mesh, in_specs=in_specs, out_specs=out_specs, check_vma=False
    )
```
